32 devices in a mesh: pair: 2 (over y), row: 4 (over z), col: 4 (over x, core).
Axes of the slice: x: 2, y: 2, z: 4, core: 2. Of those that a mesh axis runs over, the one named last changes fastest.
Arguments:
- voxels: float32 [2, 15, 16, 640], P(None, None, ('pair', 'row'), 'col'), parts along dimension 2, may hold values from -6 to 6
- disparity: float32 [2, 16, 640], P(None, ('pair', 'row'), 'col'), parts along dimension 1, may hold values from 0 to 192
- hidden: bfloat16 [2, 16, 640, 128], P(None, ('pair', 'row'), 'col'), parts along dimension 1, may hold values from -1 to 1
- context: bfloat16 [2, 16, 640, 384], P(None, ('pair', 'row'), 'col'), parts along dimension 1, may hold values from -6 to 6
- embed_first: float32 [15, 256], replicated, may hold values from -1.5 to 1.5
- embed_bias: float32 [256], replicated, may hold values from -4 to 4
- embed_second: bfloat16 [256, 256], replicated, may hold values from -0.375 to 0.375
- motion_weight: float32 [36, 128], replicated, may hold values from -1 to 1
- motion_scale: float32 [128], replicated, may hold values from -4 to 4
- motion_bias: float32 [128], replicated, may hold values from -3 to 3
- gate_kernel: bfloat16 [3, 3, 256, 256], replicated, may hold values from -0.125 to 0.125
- candidate_kernel: bfloat16 [3, 3, 256, 128], replicated, may hold values from -0.125 to 0.125
- head_weight: bfloat16 [128], replicated, may hold values from -0.5 to 0.5
Outputs:
- new_hidden: bfloat16 [2, 16, 640, 128], P(None, ('pair', 'row'), 'col'), parts along dimension 1
- increment: float32 [2, 16, 640], P(None, ('pair', 'row'), 'col'), parts along dimension 1
The draws below stay inside these ranges and needn't reach their ends.
There are 2 independent parts, one for each index of `pair`. The reference program is written for one: setup_inputs(seed, part) draws one part's arguments, and reference() takes and returns one part's arrays. A program takes and returns all parts, laid end to end along the dimension named above; an argument that names none is the same for every part. Nothing has to cross between parts.
All inputs are finite; a program needn't handle non-finite values.
Results may differ from the reference program's by a relative error of at most 0.0085.
Values may be sent and summed in bfloat16 or wider, within the bound.
A program may use at most 128 MiB of HBM per device.

```python
import jax
import jax.numpy as jnp
from jax import lax

C = 256
HID = 128
BINS = 15
LEVELS = 4
RADIUS = 4
TAPS = 9
MAXDISP = 192
H = 8
W = 640


def block_scale(rng, shape, shards, least, top_value):
    def one(dim, parts):
        draws = jax.random.uniform(jax.random.fold_in(jax.random.fold_in(rng, 6), dim), (parts,), jnp.float32, least / len(shards), top_value / len(shards))
        return jnp.repeat(jnp.exp(draws), shape[dim] // parts).reshape((-1,) + (1,) * (len(shape) - dim - 1))

    gain = one(*shards[0])
    for cut in shards[1:]:
        gain = gain * one(*cut)
    return gain


def scatter_about(own_key, extent, spread, reach, split=(), held_as=jnp.bfloat16):
    gain = block_scale(own_key, extent, split, -0.22, 0.18) if split else 1.0
    values = jax.random.normal(own_key, extent, jnp.float32) * spread * gain
    return jnp.minimum(jnp.maximum(values, -reach), reach).astype(held_as)


def setup_inputs(seed: int = 0, part: int = 0) -> dict:
    key_list = jax.random.split(jax.random.key(seed), 14)
    own_keys = jax.random.split(jax.random.fold_in(key_list[13], part), 14)
    return {
        "voxels": scatter_about(own_keys[0], (2, BINS, H, W), 1.0, 6.0, ((2, 4), (3, 4)), jnp.float32),
        "disparity": jnp.clip(192.0 * jax.random.uniform(own_keys[1], (2, H, W), jnp.float32) ** block_scale(own_keys[1], (2, H, W), ((1, 4), (2, 4)), -0.2, 0.2), 0.0, 192.0),
        "hidden": jnp.clip(jax.random.uniform(own_keys[2], (2, H, W, HID), jnp.float32, -1.0, 1.0) * block_scale(own_keys[2], (2, H, W, HID), ((1, 4), (2, 4)), -0.4, 0.0), -1.0, 1.0).astype(jnp.bfloat16),
        "context": scatter_about(own_keys[3], (2, H, W, 3 * HID), 1.0, 6.0, ((1, 4), (2, 4))),
        "embed_first": scatter_about(key_list[4], (BINS, C), BINS ** -0.5, 1.5, (), jnp.float32),
        "embed_bias": scatter_about(key_list[5], (C,), 1.0, 4.0, (), jnp.float32),
        "embed_second": scatter_about(key_list[6], (C, C), C ** -0.5, 0.375),
        "motion_weight": scatter_about(key_list[7], (LEVELS * TAPS, HID), (LEVELS * TAPS) ** -0.5, 1.0, (), jnp.float32),
        "motion_scale": scatter_about(key_list[8], (HID,), 1.0, 4.0, (), jnp.float32),
        "motion_bias": scatter_about(key_list[9], (HID,), 0.5, 3.0, (), jnp.float32),
        "gate_kernel": scatter_about(key_list[10], (3, 3, 2 * HID, 2 * HID), (18 * HID) ** -0.5, 0.125),
        "candidate_kernel": scatter_about(key_list[11], (3, 3, 2 * HID, HID), (18 * HID) ** -0.5, 0.125),
        "head_weight": scatter_about(key_list[12], (HID,), HID ** -0.5, 0.5),
    }


def encode(grid, embed_first, embed_bias, embed_second):
    first_layer = jnp.einsum("bhw,bc->hwc", grid, embed_first, precision=lax.Precision.HIGHEST)
    first_layer = jax.nn.silu(first_layer + embed_bias).astype(jnp.bfloat16)
    return jnp.dot(first_layer, embed_second, preferred_element_type=jnp.float32).astype(jnp.bfloat16)


def pyramid(scores):
    levels = [scores]
    for level_at in range(1, LEVELS):
        finer = levels[-1]
        paired = finer.reshape(finer.shape[:-1] + (finer.shape[-1] // 2, 2))
        levels.append((paired[..., 0] + paired[..., 1]) * 0.5)
    return levels


def pick(source, index, length):
    inside = (index >= 0) & (index < length)
    place = jnp.clip(index, 0, length - 1)
    value = jnp.take_along_axis(source, place[..., None], axis=-1)[..., 0]
    return jnp.where(inside, value, 0.0)


def sample(levels, position, offsets):
    gathered = []
    for level_at in range(LEVELS):
        source = levels[level_at]
        length = source.shape[-1]
        factor = 1.0 / (2 ** level_at)
        centre = position * factor - offsets * factor
        for tap_index in range(2 * RADIUS + 1):
            spot = centre + float(tap_index - RADIUS)
            floor_value = jnp.floor(spot)
            weight = spot - floor_value
            lower = floor_value.astype(jnp.int32)
            gathered.append((1.0 - weight) * pick(source, lower, length) + weight * pick(source, lower + 1, length))
    return jnp.stack(gathered, axis=-1)


def convolve(padded, kernel, row_count, col_count):
    summed = jnp.zeros((row_count, col_count, kernel.shape[-1]), jnp.float32)
    for row_shift in range(3):
        for col_shift in range(3):
            window = padded[row_shift:row_shift + row_count, col_shift:col_shift + col_count]
            summed = summed + jnp.dot(window, kernel[row_shift, col_shift], preferred_element_type=jnp.float32)
    return summed


def surround(field):
    return jnp.pad(field, ((1, 1), (1, 1), (0, 0)))


def update(query, match, offsets, state, context, motion_weight, motion_scale, motion_bias, gate_kernel, candidate_kernel, head_weight):
    row_count, col_count, channels = query.shape
    units = state.shape[-1]
    scores = jnp.einsum("yxc,ypc->yxp", query.astype(jnp.float32), match.astype(jnp.float32), precision=lax.Precision.HIGHEST)
    scores = scores * (channels ** -0.5)
    levels = pyramid(scores)
    position = jnp.arange(col_count).astype(jnp.float32)
    lookups = sample(levels, position, offsets)
    motion = jnp.dot(lookups, motion_weight, precision=lax.Precision.HIGHEST)
    motion = jax.nn.silu(motion + (offsets / MAXDISP)[..., None] * motion_scale + motion_bias).astype(jnp.bfloat16)
    gate_input = jnp.concatenate([state, motion], axis=-1)
    gate_terms = convolve(surround(gate_input), gate_kernel, row_count, col_count)
    update_gate = jax.nn.sigmoid(gate_terms[..., :units] + context[..., :units].astype(jnp.float32))
    reset_gate = jax.nn.sigmoid(gate_terms[..., units:] + context[..., units:2 * units].astype(jnp.float32))
    reset_state = (reset_gate * state.astype(jnp.float32)).astype(jnp.bfloat16)
    candidate_input = jnp.concatenate([reset_state, motion], axis=-1)
    candidate = jnp.tanh(convolve(surround(candidate_input), candidate_kernel, row_count, col_count) + context[..., 2 * units:].astype(jnp.float32))
    updated = ((1.0 - update_gate) * state.astype(jnp.float32) + update_gate * candidate).astype(jnp.bfloat16)
    return updated, jnp.dot(updated, head_weight, preferred_element_type=jnp.float32)


def mirror(array):
    return jnp.flip(array, axis=1)


def reference(voxels, disparity, hidden, context, embed_first, embed_bias, embed_second, motion_weight, motion_scale, motion_bias, gate_kernel, candidate_kernel, head_weight):
    left_features = encode(voxels[0], embed_first, embed_bias, embed_second)
    right_features = encode(voxels[1], embed_first, embed_bias, embed_second)
    weights = (motion_weight, motion_scale, motion_bias, gate_kernel, candidate_kernel, head_weight)
    left_state, left_step = update(left_features, right_features, disparity[0], hidden[0], context[0], *weights)
    right_state, right_step = update(mirror(right_features), mirror(left_features), mirror(disparity[1]), mirror(hidden[1]), mirror(context[1]), *weights)
    new_hidden = jnp.stack([left_state, mirror(right_state)])
    increment = jnp.stack([left_step, mirror(right_step)])
    return new_hidden, increment
```

```python
import functools

import jax
import jax.numpy as jnp
import numpy as np
from jax import lax
from jax.experimental import pallas as pl
from jax.experimental.pallas import tpu as pltpu
from jax.sharding import PartitionSpec as P

LEVELS = 4
RADIUS = 4
TAPS = 2 * RADIUS + 1
MAXDISP = 192


def pooling(length):
    table = np.zeros((length, length), np.float32)
    start = 0
    for level in range(1, LEVELS):
        group = 2**level
        for entry in range(length // group):
            table[entry * group : (entry + 1) * group, start + entry] = 1.0 / group
        start += length // group
    return jnp.asarray(table, jnp.bfloat16)


def split(values):
    high = lax.reduce_precision(values, 8, 7)
    return high.astype(jnp.bfloat16), (values - high).astype(jnp.bfloat16)


def silu_half(half):
    return half + half * jnp.tanh(half)


def dot(left, right):
    return jnp.dot(left, right, preferred_element_type=jnp.float32)


def encode_block(packed, first, second):
    stacked = jnp.concatenate([packed, packed[:16]], axis=0)
    half = lax.dot_general(stacked, first, (((0,), (0,)), ((), ())), preferred_element_type=jnp.float32)
    return dot(silu_half(half).astype(jnp.bfloat16), second).astype(jnp.bfloat16)


def lookup_plan(view, centre, width_all):
    lane = lax.broadcasted_iota(jnp.int32, (1, 128), 1)
    upper = lane >= 64
    slot = lane & 63
    level = sum((slot >= TAPS * l).astype(jnp.int32) for l in range(1, LEVELS))
    tap = slot - TAPS * level - RADIUS + upper.astype(jnp.int32)

    def by_level(values, dtype):
        out = jnp.full((1, 128), values[0], dtype)
        for l in range(1, LEVELS):
            out = jnp.where(level >= l, jnp.asarray(values[l], dtype), out)
        return out

    factor = by_level([1.0 / 2**l for l in range(LEVELS)], jnp.float32)
    length = by_level([width_all >> l for l in range(LEVELS)], jnp.int32)
    group = by_level([1 << 20, 128, 64, 32], jnp.int32)
    offset = by_level([0, width_all, width_all + 128, width_all + 192], jnp.int32)
    shrink = by_level([0, 0, 64, 96], jnp.int32)
    spot = centre * factor
    floor_value = jnp.floor(spot)
    weight = spot - floor_value
    weight = jnp.where(upper, weight, 1.0 - weight)
    index = floor_value.astype(jnp.int32) + tap
    inside = (index >= 0) & (index < length) & (slot < LEVELS * TAPS)
    weight = jnp.where(inside, weight, 0.0)
    index = jnp.minimum(jnp.maximum(index, 0), length - 1)
    if view:
        index = length - 1 - index
    block = (index >= group).astype(jnp.int32) + (index >= 2 * group).astype(jnp.int32)
    place = offset + index - block * jnp.where(level > 0, group, 0) + 256 * block
    place = place - jnp.where(block == 2, shrink, 0)
    return place, weight


def motion_of(view, query, match, disparity, position, pool, pool_last, weights, scale_bias):
    width_all = match.shape[0]
    scores = lax.dot_general(query, match, (((1,), (1,)), ((), ())), preferred_element_type=jnp.float32)
    rounded = scores.astype(jnp.bfloat16)
    pieces = [scores[:, at : at + 128] for at in range(0, width_all, 128)]
    for at in range(0, width_all - 255, 256):
        pooled = dot(rounded[:, at : at + 256], pool)
        pieces += [pooled[:, :128], pooled[:, 128:]]
    pieces.append(dot(rounded[:, width_all - 128 :], pool_last))
    place, weight = lookup_plan(view, position - disparity, width_all)
    lane = place & 127
    block = place >> 7
    taken = jnp.zeros_like(weight)
    for at, piece in enumerate(pieces):
        values = jnp.take_along_axis(piece, lane, axis=1, mode="promise_in_bounds")
        taken = jnp.where(block == at, values, taken)
    taken = taken * weight
    high = taken.astype(jnp.bfloat16)
    low = (taken - high.astype(jnp.float32)).astype(jnp.bfloat16)
    both = dot(jnp.concatenate([high, low], axis=1), weights)
    half = both[:, :128] + both[:, 128:] + disparity * scale_bias[0:1] + scale_bias[1:2]
    return silu_half(half)


def motion_kernel(packed_ref, disp_ref, first_ref, second_ref, pool_ref, last_ref, weights_ref, sb_ref, out_ref, feat):
    count, _, pixels = packed_ref.shape
    cols = pixels // 4
    me = lax.axis_index("col")
    for j in range(count):
        block = encode_block(packed_ref[j], first_ref[...], second_ref[...])
        for k in range(4):
            feat[k, j * cols : (j + 1) * cols, :] = block[k * cols : (k + 1) * cols]
    disparity = disp_ref[...].T
    own = me * cols + lax.broadcasted_iota(jnp.int32, (cols, 1), 0)
    for k in range(4):
        view = k // 2
        query = feat[k, pl.ds(pl.multiple_of(me * cols, 32), cols), :] * jnp.bfloat16(1.0 / 16)
        position = (count * cols - 1 - own if view else own).astype(jnp.float32)
        motion = motion_of(
            view, query, feat[k ^ 2], disparity[:cols, k : k + 1], position,
            pool_ref[...], last_ref[...], weights_ref[...], sb_ref[...],
        )
        out_ref[k * cols : (k + 1) * cols, :] = motion.astype(jnp.bfloat16)


def pack_inputs(voxels, disparity, embed_first, embed_bias, motion_weight, motion_scale, motion_bias):
    bins = voxels.shape[1]
    cols = voxels.shape[3]
    flat = voxels.transpose(1, 0, 2, 3).reshape(bins, -1)
    flat = jnp.concatenate([flat, jnp.ones((16 - bins, flat.shape[1]), flat.dtype)], axis=0)
    packed = jnp.concatenate(split(flat), axis=0)
    first = jnp.concatenate([embed_first, embed_bias[None]], axis=0) * 0.5
    first_high, first_low = split(first)
    first = jnp.concatenate([first_high, first_high, first_low], axis=0)
    disp = jnp.pad(disparity.reshape(4, cols), ((0, 4), (0, 256 - cols)))
    weight = jnp.pad(motion_weight * 0.5, ((0, 64 - motion_weight.shape[0]), (0, 0)))
    high, low = split(jnp.concatenate([weight, weight], axis=0))
    weights = jnp.concatenate(
        [jnp.concatenate([high, low], axis=1), jnp.concatenate([high, jnp.zeros_like(low)], axis=1)], axis=0
    )
    scale_bias = jnp.stack([motion_scale * (0.5 / MAXDISP), motion_bias * 0.5])
    return packed, disp, first, weights, scale_bias


def extended(shard, sides, width):
    for axis, dim in sides:
        size, length = (lax.axis_size(axis), shard.shape[dim])
        up = [(i, (i + 1) % size) for i in range(size - 1)]
        down = [(j, i) for i, j in up]
        last = lax.slice_in_dim(shard, length - width, length, axis=dim)
        initial = lax.slice_in_dim(shard, 0, width, axis=dim)
        before = lax.ppermute(last, axis, up)
        after = lax.ppermute(initial, axis, down)
        shard = jnp.concatenate([before, shard, after], axis=dim)
    return shard


def convolve(padded, kernel, row_count, col_count):
    windows = []
    for row_shift in range(3):
        for col_shift in range(3):
            windows.append(
                padded[:, row_shift : row_shift + row_count, col_shift : col_shift + col_count]
            )
    stacked_input = jnp.concatenate(windows, axis=-1)
    depth = 9 * kernel.shape[2]
    flat_kernel = kernel.reshape(depth, kernel.shape[-1])
    mirror_flat = kernel[:, ::-1].reshape(depth, kernel.shape[-1])
    both_kernels = jnp.stack([flat_kernel, mirror_flat])
    return jnp.einsum(
        "vyxk,vkd->vyxd", stacked_input, both_kernels, preferred_element_type=jnp.float32
    )


def local(
    voxels,
    disparity,
    hidden,
    context,
    embed_first,
    embed_bias,
    embed_second,
    motion_weight,
    motion_scale,
    motion_bias,
    gate_kernel,
    candidate_kernel,
    head_weight,
):
    row_count = hidden.shape[1]
    col_count = hidden.shape[2]
    units = hidden.shape[-1]
    packed, disp, first, weights, scale_bias = pack_inputs(
        voxels, disparity, embed_first, embed_bias, motion_weight, motion_scale, motion_bias
    )
    gathered = lax.all_gather(packed, "col", axis=0)
    count = gathered.shape[0]
    motion = pl.pallas_call(
        motion_kernel,
        out_shape=jax.ShapeDtypeStruct((4 * col_count, units), jnp.bfloat16),
        in_specs=[pl.BlockSpec(memory_space=pltpu.VMEM)] * 8,
        out_specs=pl.BlockSpec(memory_space=pltpu.VMEM),
        scratch_shapes=[pltpu.VMEM((4, count * col_count, 256), jnp.bfloat16)],
        compiler_params=pltpu.CompilerParams(vmem_limit_bytes=40 * 2**20),
    )(gathered, disp, first, embed_second, pooling(256), pooling(128), weights, scale_bias)
    motion = motion.reshape(hidden.shape)
    gate_input = jnp.concatenate([hidden, motion], axis=-1)
    gate_padded = extended(gate_input, (("row", 1), ("col", 2)), 1)
    motion_padded = gate_padded[..., units:]
    gate_terms = convolve(gate_padded, gate_kernel, row_count, col_count)
    update_gate = jax.nn.sigmoid(gate_terms[..., :units] + context[..., :units].astype(jnp.float32))
    reset_gate = jax.nn.sigmoid(
        gate_terms[..., units:] + context[..., units : 2 * units].astype(jnp.float32)
    )
    reset_state = (reset_gate * hidden.astype(jnp.float32)).astype(jnp.bfloat16)
    reset_padded = extended(reset_state, (("row", 1), ("col", 2)), 1)
    candidate_padded = jnp.concatenate([reset_padded, motion_padded], axis=-1)
    candidate = jnp.tanh(
        convolve(candidate_padded, candidate_kernel, row_count, col_count)
        + context[..., 2 * units :].astype(jnp.float32)
    )
    updated = ((1.0 - update_gate) * hidden.astype(jnp.float32) + update_gate * candidate).astype(
        jnp.bfloat16
    )
    increment = jnp.dot(updated, head_weight, preferred_element_type=jnp.float32)
    return (updated, increment)


def solution(mesh):
    tile = P(None, ("pair", "row"), "col")
    in_specs = (P(None, None, ("pair", "row"), "col"),) + (tile,) * 3 + (P(),) * 9
    return jax.shard_map(local, mesh=mesh, in_specs=in_specs, out_specs=(tile, tile), check_vma=False)
```

```python
import functools

import jax
import jax.numpy as jnp
from jax import lax
from jax.experimental import pallas as pl
from jax.experimental.pallas import tpu as pltpu
from jax.sharding import PartitionSpec as P

LEVELS = 4
RADIUS = 4
TAPS = 2 * RADIUS + 1
MAXDISP = 192


def pooling(length):
    row = lax.broadcasted_iota(jnp.int32, (length, length), 0)
    column = lax.broadcasted_iota(jnp.int32, (length, length), 1)
    table = jnp.zeros((length, length), jnp.float32)
    start = 0
    for level in range(1, LEVELS):
        entries = length >> level
        hit = ((row >> level) == column - start) & (column >= start) & (column < start + entries)
        table = jnp.where(hit, 1.0 / 2**level, table)
        start += entries
    return table.astype(jnp.bfloat16)


def split(values):
    high = values.astype(jnp.bfloat16)
    return high, (values - high.astype(jnp.float32)).astype(jnp.bfloat16)


def silu_half(half):
    return half + half * jnp.tanh(half)


def dot(left, right):
    return jnp.dot(left, right, preferred_element_type=jnp.float32)


def encode_block(packed, first, second):
    stacked = jnp.concatenate([packed, packed[:16]], axis=0)
    half = lax.dot_general(stacked, first, (((0,), (0,)), ((), ())), preferred_element_type=jnp.float32)
    return dot(silu_half(half).astype(jnp.bfloat16), second).astype(jnp.bfloat16)


def lookup_plan(view, centre, width_all):
    lane = lax.broadcasted_iota(jnp.int32, (1, 128), 1)
    upper = lane >= 64
    slot = lane & 63
    level = sum((slot >= TAPS * l).astype(jnp.int32) for l in range(1, LEVELS))
    tap = slot - TAPS * level - RADIUS + upper.astype(jnp.int32)

    def by_level(values, dtype):
        out = jnp.full((1, 128), values[0], dtype)
        for l in range(1, LEVELS):
            out = jnp.where(level >= l, jnp.asarray(values[l], dtype), out)
        return out

    factor = by_level([1.0 / 2**l for l in range(LEVELS)], jnp.float32)
    length = by_level([width_all >> l for l in range(LEVELS)], jnp.int32)
    group = by_level([1 << 20, 128, 64, 32], jnp.int32)
    offset = by_level([0, width_all, width_all + 128, width_all + 192], jnp.int32)
    shrink = by_level([0, 0, 64, 96], jnp.int32)
    spot = centre * factor
    floor_value = jnp.floor(spot)
    weight = spot - floor_value
    weight = jnp.where(upper, weight, 1.0 - weight)
    index = floor_value.astype(jnp.int32) + tap
    inside = (index >= 0) & (index < length) & (slot < LEVELS * TAPS)
    weight = jnp.where(inside, weight, 0.0)
    index = jnp.minimum(jnp.maximum(index, 0), length - 1)
    if view:
        index = length - 1 - index
    block = (index >= group).astype(jnp.int32) + (index >= 2 * group).astype(jnp.int32)
    place = offset + index - block * jnp.where(level > 0, group, 0) + 256 * block
    place = place - jnp.where(block == 2, shrink, 0)
    return place, weight


def motion_of(view, query, match, disparity, position, pool, pool_last, weights, scale_bias):
    width_all = match.shape[0]
    scores = lax.dot_general(query, match, (((1,), (1,)), ((), ())), preferred_element_type=jnp.float32)
    rounded = scores.astype(jnp.bfloat16)
    pieces = [scores[:, at : at + 128] for at in range(0, width_all, 128)]
    for at in range(0, width_all - 255, 256):
        pooled = dot(rounded[:, at : at + 256], pool)
        pieces += [pooled[:, :128], pooled[:, 128:]]
    pieces.append(dot(rounded[:, width_all - 128 :], pool_last))
    place, weight = lookup_plan(view, position - disparity, width_all)
    lane = place & 127
    block = place >> 7
    taken = jnp.zeros_like(weight)
    for at, piece in enumerate(pieces):
        values = jnp.take_along_axis(piece, lane, axis=1, mode="promise_in_bounds")
        taken = jnp.where(block == at, values, taken)
    taken = taken * weight
    high = taken.astype(jnp.bfloat16)
    low = (taken - high.astype(jnp.float32)).astype(jnp.bfloat16)
    both = dot(jnp.concatenate([high, low], axis=1), weights)
    half = both[:, :128] + both[:, 128:] + disparity * scale_bias[0:1] + scale_bias[1:2]
    return silu_half(half)


DIRECTIONS = ((-1, 0), (1, 0), (0, -1), (0, 1), (-1, -1), (-1, 1), (1, -1), (1, 1))
EDGE = 16


def sigmoid(values):
    return 0.5 + 0.5 * jnp.tanh(0.5 * values)


def update_kernel(
    voxels_ref, disparity_ref, hidden_ref, context_hbm, first_ref, bias_ref, second_ref, weight_ref, scale_ref,
    shift_ref, gate_hbm, cand_hbm, head_ref,
    out_ref, step_ref,
    context, gate, cand, packed, arrived, first16, feat, weight64, disp8,
    motion, reset, rows_in, sides_in, wide, update,
    local_sem, gather_send, gather_recv, halo_send, halo_recv,
):
    views, bins, row_count, cols = voxels_ref.shape
    units = hidden_ref.shape[-1]
    count, bands = lax.axis_size("col"), lax.axis_size("row")
    me, band = lax.axis_index("col"), lax.axis_index("row")

    loads = [
        pltpu.make_async_copy(source, target, local_sem.at[at])
        for at, (source, target) in enumerate(((gate_hbm, gate), (context_hbm, context), (cand_hbm, cand)))
    ]
    for load in loads:
        load.start()

    def inside(dy, dx):
        row, col = band + dy, me + dx
        return (row >= 0) & (row < bands) & (col >= 0) & (col < count)

    barrier = pltpu.get_barrier_semaphore()
    expected = jnp.int32(count - 1)
    for d in range(1, count):
        pl.semaphore_signal(
            barrier, inc=1, device_id={"row": band, "col": lax.rem(me + d, count)}, device_id_type=pl.DeviceIdType.MESH
        )
    for dy, dx in DIRECTIONS:
        if dy:
            there = inside(dy, dx)
            expected = expected + there.astype(jnp.int32)

            @pl.when(there)
            def _(dy=dy, dx=dx):
                pl.semaphore_signal(
                    barrier, inc=1, device_id={"row": band + dy, "col": me + dx}, device_id_type=pl.DeviceIdType.MESH
                )

    pieces = [voxels_ref[k // row_count, :, k % row_count, :] for k in range(views * row_count)]
    flat = jnp.concatenate([jnp.concatenate(pieces, axis=1), jnp.ones((16 - bins, 4 * cols), jnp.float32)], axis=0)
    high, low = split(flat)
    packed[...] = jnp.concatenate([high, low], axis=0)

    for side, dy in ((0, -1), (1, 1)):

        @pl.when(jnp.logical_not(inside(dy, 0)))
        def _(side=side):
            for turn in range(3):
                rows_in[turn, side] = jnp.zeros(rows_in.shape[2:], rows_in.dtype)

    for side, dx in ((0, -1), (1, 1)):
        for at, dy in ((0, -1), (1, 0), (row_count + 1, 1)):

            @pl.when(jnp.logical_not(inside(dy, dx)))
            def _(side=side, dy=dy, at=at):
                for turn in range(3):
                    for line in range(at, at + (1 if dy else row_count)):
                        for view in range(views):
                            sides_in[turn, side, view, line] = jnp.zeros((EDGE, units), jnp.bfloat16)

    pl.semaphore_wait(barrier, expected)

    gathers = [
        pltpu.make_async_remote_copy(
            src_ref=packed, dst_ref=arrived.at[s - 1], send_sem=gather_send.at[s - 1], recv_sem=gather_recv.at[s - 1],
            device_id={"row": band, "col": lax.rem(me + count - s, count)}, device_id_type=pl.DeviceIdType.MESH,
        )
        for s in range(1, count)
    ]
    for gather in gathers:
        gather.start()

    def halo(turn, source):
        copies = []
        for q, (dy, dx) in enumerate(DIRECTIONS):
            line = 0 if dy < 0 else row_count - 1
            span = pl.ds(0 if dx < 0 else cols - EDGE, EDGE)
            side = 1 if dx < 0 else 0
            if dx == 0:
                src, dst = source.at[:, line], rows_in.at[turn, 1 if dy < 0 else 0]
            elif dy == 0:
                src, dst = source.at[:, :, span], sides_in.at[turn, side, :, pl.ds(1, row_count)]
            else:
                src = source.at[:, line, span]
                dst = sides_in.at[turn, side, :, row_count + 1 if dy < 0 else 0]
            copies.append(
                pltpu.make_async_remote_copy(
                    src_ref=src, dst_ref=dst, send_sem=halo_send.at[turn, q], recv_sem=halo_recv.at[turn, q],
                    device_id={"row": band + dy, "col": me + dx}, device_id_type=pl.DeviceIdType.MESH,
                )
            )
        return copies

    def each(copies, action, sign):
        for copy, (dy, dx) in zip(copies, DIRECTIONS):
            pl.when(inside(sign * dy, sign * dx))(functools.partial(action, copy))

    def start(copy):
        copy.start()

    def wait_recv(copy):
        copy.wait_recv()

    def wait_send(copy):
        copy.wait_send()

    halos = [halo(turn, source) for turn, source in enumerate((hidden_ref, motion, reset))]
    each(halos[0], start, 1)

    first16[0:bins] = first_ref[...] * 0.5
    first16[bins : bins + 1] = bias_ref[...] * 0.5
    first_high, first_low = split(first16[...])
    first = jnp.concatenate([first_high, first_high, first_low], axis=0)
    weight64[...] = jnp.zeros_like(weight64)
    weight64[0 : LEVELS * TAPS] = weight_ref[...] * 0.5
    high, low = split(weight64[...])
    blank = jnp.zeros_like(low)
    weights = jnp.concatenate(
        [jnp.concatenate([high, low], axis=1)] * 2 + [jnp.concatenate([high, blank], axis=1)] * 2, axis=0
    )
    scale_bias = jnp.concatenate([scale_ref[...] * (0.5 / MAXDISP), shift_ref[...] * 0.5], axis=0)
    disp8[...] = jnp.zeros_like(disp8)
    for k in range(views * row_count):
        disp8[k : k + 1, 0:cols] = disparity_ref[k // row_count, k % row_count : k % row_count + 1, :]
    disparity = disp8[...].T
    pool, pool_last = pooling(256), pooling(128)

    for s in range(count):
        if s:
            gathers[s - 1].wait_recv()
        block = encode_block(arrived[s - 1] if s else packed[...], first, second_ref[...])
        spot = pl.ds(pl.multiple_of(lax.rem(me + s, count) * cols, 32), cols)
        for k in range(views * row_count):
            feat[k, spot, :] = block[k * cols : (k + 1) * cols]

    own = me * cols + lax.broadcasted_iota(jnp.int32, (cols, 1), 0)
    for k in range(views * row_count):
        view, line = k // row_count, k % row_count
        query = feat[k, pl.ds(pl.multiple_of(me * cols, 32), cols), :] * jnp.bfloat16(1.0 / 16)
        position = (count * cols - 1 - own if view else own).astype(jnp.float32)
        other = (views - 1 - view) * row_count + line
        motion[view, line] = motion_of(
            view, query, feat[other], disparity[:cols, k : k + 1], position, pool, pool_last, weights, scale_bias
        ).astype(jnp.bfloat16)
    each(halos[1], start, 1)

    slot = lax.broadcasted_iota(jnp.int32, (EDGE, units), 0)

    def widen(turn, source):
        for view in range(views):
            for line in range(row_count + 2):
                if line == 0:
                    centre = rows_in[turn, 0, view]
                elif line == row_count + 1:
                    centre = rows_in[turn, 1, view]
                else:
                    centre = source[view, line - 1]
                left = sides_in[turn, 0, view, line].astype(jnp.float32)
                right = sides_in[turn, 1, view, line].astype(jnp.float32)
                edge = jnp.where(slot == EDGE - 1, left, right)
                ring = jnp.concatenate([centre.astype(jnp.float32), edge], axis=0)
                before = pltpu.roll(ring, 1, axis=0)[:cols]
                after = pltpu.roll(ring, cols + EDGE - 1, axis=0)[:cols]
                wide[turn, view, line, :, 0:units] = before.astype(jnp.bfloat16)
                wide[turn, view, line, :, units : 2 * units] = centre
                wide[turn, view, line, :, 2 * units :] = after.astype(jnp.bfloat16)

    def convolve(turn, view, kernel, part):
        total = None
        order = (2, 1, 0) if view else (0, 1, 2)
        for a in range(3):
            window = wide[turn, view, a : a + row_count].reshape(row_count * cols, 3 * units)
            taps = jnp.concatenate([kernel[a, b, part * units : (part + 1) * units, :] for b in order], axis=0)
            term = dot(window, taps)
            total = term if total is None else total + term
        return total

    each(halos[0], wait_recv, -1)
    widen(0, hidden_ref)
    loads[0].wait()
    gate_terms = [convolve(0, view, gate, 0) for view in range(views)]
    loads[1].wait()
    each(halos[1], wait_recv, -1)
    widen(1, motion)
    for view in range(views):
        terms = gate_terms[view] + convolve(1, view, gate, 1)
        around = context[view, :, :, 0 : 2 * units].reshape(row_count * cols, 2 * units).astype(jnp.float32)
        gates = sigmoid(terms + around)
        update[view] = gates[:, :units]
        state = hidden_ref[view].reshape(row_count * cols, units).astype(jnp.float32)
        kept = (gates[:, units:] * state).astype(jnp.bfloat16)
        reset[view] = kept.reshape(row_count, cols, units)
    each(halos[2], start, 1)
    loads[2].wait()
    cand_terms = [convolve(1, view, cand, 1) for view in range(views)]
    each(halos[2], wait_recv, -1)
    widen(2, reset)
    for view in range(views):
        terms = cand_terms[view] + convolve(2, view, cand, 0)
        around = context[view, :, :, 2 * units :].reshape(row_count * cols, units).astype(jnp.float32)
        candidate = jnp.tanh(terms + around)
        state = hidden_ref[view].reshape(row_count * cols, units).astype(jnp.float32)
        opened = update[view]
        updated = ((1.0 - opened) * state + opened * candidate).astype(jnp.bfloat16)
        out_ref[view] = updated.reshape(row_count, cols, units)
        for line in range(row_count):
            step_ref[view, line : line + 1, :] = lax.dot_general(
                head_ref[...], updated[line * cols : (line + 1) * cols], (((1,), (1,)), ((), ())),
                preferred_element_type=jnp.float32,
            )
    for gather in gathers:
        gather.wait_send()
    for copies in halos:
        each(copies, wait_send, 1)


def local(
    voxels, disparity, hidden, context, embed_first, embed_bias, embed_second, motion_weight, motion_scale,
    motion_bias, gate_kernel, candidate_kernel, head_weight,
):
    views, bins, row_count, cols = voxels.shape
    units = hidden.shape[-1]
    channels = embed_second.shape[0]
    count = lax.axis_size("col")
    pixels = views * row_count * cols
    vmem = pl.BlockSpec(memory_space=pltpu.VMEM)
    anywhere = pl.BlockSpec(memory_space=pl.ANY)
    return pl.pallas_call(
        update_kernel,
        out_shape=(
            jax.ShapeDtypeStruct(hidden.shape, jnp.bfloat16),
            jax.ShapeDtypeStruct(disparity.shape, jnp.float32),
        ),
        in_specs=[vmem] * 3 + [anywhere] + [vmem] * 6 + [anywhere] * 2 + [vmem],
        out_specs=(vmem, vmem),
        scratch_shapes=[
            pltpu.VMEM(context.shape, jnp.bfloat16),
            pltpu.VMEM(gate_kernel.shape, jnp.bfloat16),
            pltpu.VMEM(candidate_kernel.shape, jnp.bfloat16),
            pltpu.VMEM((32, pixels), jnp.bfloat16),
            pltpu.VMEM((count - 1, 32, pixels), jnp.bfloat16),
            pltpu.VMEM((16, channels), jnp.float32),
            pltpu.VMEM((views * row_count, count * cols, channels), jnp.bfloat16),
            pltpu.VMEM((64, units), jnp.float32),
            pltpu.VMEM((8, 256), jnp.float32),
            pltpu.VMEM(hidden.shape, jnp.bfloat16),
            pltpu.VMEM(hidden.shape, jnp.bfloat16),
            pltpu.VMEM((3, 2, views, cols, units), jnp.bfloat16),
            pltpu.VMEM((3, 2, views, row_count + 2, EDGE, units), jnp.bfloat16),
            pltpu.VMEM((3, views, row_count + 2, cols, 3 * units), jnp.bfloat16),
            pltpu.VMEM((views, row_count * cols, units), jnp.float32),
            pltpu.SemaphoreType.DMA((3,)),
            pltpu.SemaphoreType.DMA((count - 1,)),
            pltpu.SemaphoreType.DMA((count - 1,)),
            pltpu.SemaphoreType.DMA((3, 8)),
            pltpu.SemaphoreType.DMA((3, 8)),
        ],
        compiler_params=pltpu.CompilerParams(
            collective_id=0, has_side_effects=True, vmem_limit_bytes=48 * 2**20
        ),
    )(
        voxels, disparity, hidden, context, embed_first, embed_bias[None], embed_second, motion_weight,
        motion_scale[None], motion_bias[None], gate_kernel, candidate_kernel, head_weight[None],
    )


def solution(mesh):
    tile = P(None, ("pair", "row"), "col")
    in_specs = (P(None, None, ("pair", "row"), "col"),) + (tile,) * 3 + (P(),) * 9
    return jax.shard_map(local, mesh=mesh, in_specs=in_specs, out_specs=(tile, tile), check_vma=False)
```

```python
import functools

import jax
import jax.numpy as jnp
from jax import lax
from jax.experimental import pallas as pl
from jax.experimental.pallas import tpu as pltpu
from jax.sharding import PartitionSpec as P

LEVELS = 4
RADIUS = 4
TAPS = 2 * RADIUS + 1
MAXDISP = 192


def pooling(length):
    row = lax.broadcasted_iota(jnp.int32, (length, length), 0)
    column = lax.broadcasted_iota(jnp.int32, (length, length), 1)
    table = jnp.zeros((length, length), jnp.float32)
    start = 0
    for level in range(1, LEVELS):
        entries = length >> level
        hit = ((row >> level) == column - start) & (column >= start) & (column < start + entries)
        table = jnp.where(hit, 1.0 / 2**level, table)
        start += entries
    return table.astype(jnp.bfloat16)


def split(values):
    high = values.astype(jnp.bfloat16)
    return high, (values - high.astype(jnp.float32)).astype(jnp.bfloat16)


def silu_half(half):
    return half + half * jnp.tanh(half)


def dot(left, right):
    return jnp.dot(left, right, preferred_element_type=jnp.float32)


def encode_block(packed, first, second):
    stacked = jnp.concatenate([packed, packed[:16]], axis=0)
    half = lax.dot_general(stacked, first, (((0,), (0,)), ((), ())), preferred_element_type=jnp.float32)
    return dot(silu_half(half).astype(jnp.bfloat16), second).astype(jnp.bfloat16)


def lookup_plan(view, centre, width_all):
    lane = lax.broadcasted_iota(jnp.int32, (1, 128), 1)
    upper = lane >= 64
    slot = lane & 63
    level = sum((slot >= TAPS * l).astype(jnp.int32) for l in range(1, LEVELS))
    tap = slot - TAPS * level - RADIUS + upper.astype(jnp.int32)

    def by_level(values, dtype):
        out = jnp.full((1, 128), values[0], dtype)
        for l in range(1, LEVELS):
            out = jnp.where(level >= l, jnp.asarray(values[l], dtype), out)
        return out

    factor = by_level([1.0 / 2**l for l in range(LEVELS)], jnp.float32)
    length = by_level([width_all >> l for l in range(LEVELS)], jnp.int32)
    group = by_level([1 << 20, 128, 64, 32], jnp.int32)
    offset = by_level([0, width_all, width_all + 128, width_all + 192], jnp.int32)
    shrink = by_level([0, 0, 64, 96], jnp.int32)
    spot = centre * factor
    floor_value = jnp.floor(spot)
    weight = spot - floor_value
    weight = jnp.where(upper, weight, 1.0 - weight)
    index = floor_value.astype(jnp.int32) + tap
    inside = (index >= 0) & (index < length) & (slot < LEVELS * TAPS)
    weight = jnp.where(inside, weight, 0.0)
    index = jnp.minimum(jnp.maximum(index, 0), length - 1)
    if view:
        index = length - 1 - index
    block = (index >= group).astype(jnp.int32) + (index >= 2 * group).astype(jnp.int32)
    place = offset + index - block * jnp.where(level > 0, group, 0) + 256 * block
    place = place - jnp.where(block == 2, shrink, 0)
    return place, weight


def motion_of(view, query, match, disparity, position, pool, pool_last, weights, scale_bias):
    width_all = match.shape[0]
    scores = lax.dot_general(query, match, (((1,), (1,)), ((), ())), preferred_element_type=jnp.float32)
    rounded = scores.astype(jnp.bfloat16)
    pieces = [scores[:, at : at + 128] for at in range(0, width_all, 128)]
    for at in range(0, width_all - 255, 256):
        pooled = dot(rounded[:, at : at + 256], pool)
        pieces += [pooled[:, :128], pooled[:, 128:]]
    pieces.append(dot(rounded[:, width_all - 128 :], pool_last))
    place, weight = lookup_plan(view, position - disparity, width_all)
    lane = place & 127
    block = place >> 7
    taken = jnp.zeros_like(weight)
    for at, piece in enumerate(pieces):
        values = jnp.take_along_axis(piece, lane, axis=1, mode="promise_in_bounds")
        taken = jnp.where(block == at, values, taken)
    taken = taken * weight
    high = taken.astype(jnp.bfloat16)
    low = (taken - high.astype(jnp.float32)).astype(jnp.bfloat16)
    both = dot(jnp.concatenate([high, low], axis=1), weights)
    half = both[:, :128] + both[:, 128:] + disparity * scale_bias[0:1] + scale_bias[1:2]
    return silu_half(half)


DIRECTIONS = ((-1, 0), (1, 0), (0, -1), (0, 1), (-1, -1), (-1, 1), (1, -1), (1, 1))
EDGE = 16


def sigmoid(values):
    return 0.5 + 0.5 * jnp.tanh(0.5 * values)


def update_kernel(
    voxels_hbm, disparity_hbm, hidden_hbm, context_hbm, first_hbm, bias_hbm, second_hbm, weight_hbm, scale_hbm,
    shift_hbm, gate_hbm, cand_hbm, head_hbm,
    out_ref, step_ref,
    voxels_ref, disparity_ref, hidden_ref, context, first_ref, bias_ref, second_ref, weight_ref, scale_ref,
    shift_ref, gate, cand, head_ref,
    packed, arrived, first16, feat, weight64, disp8,
    motion, reset, rows_in, sides_in, wide,
    local_sem, gather_send, gather_recv, halo_send, halo_recv,
):
    views, bins, row_count, cols = voxels_ref.shape
    units = hidden_ref.shape[-1]
    count, bands = lax.axis_size("col"), lax.axis_size("row")
    me, band = lax.axis_index("col"), lax.axis_index("row")

    pairs = {
        "voxels": (voxels_hbm, voxels_ref), "first": (first_hbm, first_ref), "bias": (bias_hbm, bias_ref),
        "second": (second_hbm, second_ref), "weight": (weight_hbm, weight_ref), "scale": (scale_hbm, scale_ref),
        "shift": (shift_hbm, shift_ref), "disparity": (disparity_hbm, disparity_ref),
        "hidden": (hidden_hbm, hidden_ref), "gate": (gate_hbm, gate), "context": (context_hbm, context),
        "cand": (cand_hbm, cand), "head": (head_hbm, head_ref),
    }
    loads = {
        name: pltpu.make_async_copy(source, target, local_sem.at[at])
        for at, (name, (source, target)) in enumerate(pairs.items())
    }
    loads["voxels"].start()

    def inside(dy, dx):
        row, col = band + dy, me + dx
        return (row >= 0) & (row < bands) & (col >= 0) & (col < count)

    barrier = pltpu.get_barrier_semaphore()
    expected = jnp.int32(count - 1)
    for d in range(1, count):
        pl.semaphore_signal(
            barrier, inc=1, device_id={"row": band, "col": lax.rem(me + d, count)}, device_id_type=pl.DeviceIdType.MESH
        )
    for dy, dx in DIRECTIONS:
        if dy:
            there = inside(dy, dx)
            expected = expected + there.astype(jnp.int32)

            @pl.when(there)
            def _(dy=dy, dx=dx):
                pl.semaphore_signal(
                    barrier, inc=1, device_id={"row": band + dy, "col": me + dx}, device_id_type=pl.DeviceIdType.MESH
                )

    for name in list(pairs)[1:]:
        loads[name].start()
    loads["voxels"].wait()

    pieces = [voxels_ref[k // row_count, :, k % row_count, :] for k in range(views * row_count)]
    flat = jnp.concatenate([jnp.concatenate(pieces, axis=1), jnp.ones((16 - bins, 4 * cols), jnp.float32)], axis=0)
    high, low = split(flat)
    packed[...] = jnp.concatenate([high, low], axis=0)

    for side, dy in ((0, -1), (1, 1)):

        @pl.when(jnp.logical_not(inside(dy, 0)))
        def _(side=side):
            for turn in range(3):
                rows_in[turn, side] = jnp.zeros(rows_in.shape[2:], rows_in.dtype)

    for side, dx in ((0, -1), (1, 1)):
        for at, dy in ((0, -1), (1, 0), (row_count + 1, 1)):

            @pl.when(jnp.logical_not(inside(dy, dx)))
            def _(side=side, dy=dy, at=at):
                for turn in range(3):
                    for line in range(at, at + (1 if dy else row_count)):
                        for view in range(views):
                            sides_in[turn, side, view, line] = jnp.zeros((EDGE, units), jnp.bfloat16)

    pl.semaphore_wait(barrier, expected)

    gathers = [
        pltpu.make_async_remote_copy(
            src_ref=packed, dst_ref=arrived.at[s - 1], send_sem=gather_send.at[s - 1], recv_sem=gather_recv.at[s - 1],
            device_id={"row": band, "col": lax.rem(me + count - s, count)}, device_id_type=pl.DeviceIdType.MESH,
        )
        for s in range(1, count)
    ]
    for gather in gathers:
        gather.start()

    def halo(turn, view, source):
        copies = []
        for q, (dy, dx) in enumerate(DIRECTIONS):
            line = 0 if dy < 0 else row_count - 1
            span = pl.ds(0 if dx < 0 else cols - EDGE, EDGE)
            side = 1 if dx < 0 else 0
            if dx == 0:
                src, dst = source.at[view, line], rows_in.at[turn, 1 if dy < 0 else 0, view]
            elif dy == 0:
                src, dst = source.at[view, :, span], sides_in.at[turn, side, view, pl.ds(1, row_count)]
            else:
                src = source.at[view, line, span]
                dst = sides_in.at[turn, side, view, row_count + 1 if dy < 0 else 0]
            copies.append(
                pltpu.make_async_remote_copy(
                    src_ref=src, dst_ref=dst, send_sem=halo_send.at[turn, view, q],
                    recv_sem=halo_recv.at[turn, view, q],
                    device_id={"row": band + dy, "col": me + dx}, device_id_type=pl.DeviceIdType.MESH,
                )
            )
        return copies

    def each(copies, action, sign):
        for copy, (dy, dx) in zip(copies, DIRECTIONS):
            pl.when(inside(sign * dy, sign * dx))(functools.partial(action, copy))

    def start(copy):
        copy.start()

    def wait_recv(copy):
        copy.wait_recv()

    def wait_send(copy):
        copy.wait_send()

    halos = [
        [halo(turn, view, source) for view in range(views)] for turn, source in enumerate((hidden_hbm, motion, reset))
    ]
    for view in range(views):
        each(halos[0][view], start, 1)

    for name in ("first", "bias", "second", "weight", "scale", "shift", "disparity"):
        loads[name].wait()
    first16[0:bins] = first_ref[...] * 0.5
    first16[bins : bins + 1] = bias_ref[...] * 0.5
    first_high, first_low = split(first16[...])
    first = jnp.concatenate([first_high, first_high, first_low], axis=0)
    weight64[...] = jnp.zeros_like(weight64)
    weight64[0 : LEVELS * TAPS] = weight_ref[...] * 0.5
    high, low = split(weight64[...])
    blank = jnp.zeros_like(low)
    weights = jnp.concatenate(
        [jnp.concatenate([high, low], axis=1)] * 2 + [jnp.concatenate([high, blank], axis=1)] * 2, axis=0
    )
    scale_bias = jnp.concatenate([scale_ref[...] * (0.5 / MAXDISP), shift_ref[...] * 0.5], axis=0)
    disp8[...] = jnp.zeros_like(disp8)
    for k in range(views * row_count):
        disp8[k : k + 1, 0:cols] = disparity_ref[k // row_count, k % row_count : k % row_count + 1, :]
    disparity = disp8[...].T
    pool, pool_last = pooling(256), pooling(128)

    for s in range(count):
        if s:
            gathers[s - 1].wait_recv()
        block = encode_block(arrived[s - 1] if s else packed[...], first, second_ref[...])
        spot = pl.ds(pl.multiple_of(lax.rem(me + s, count) * cols, 32), cols)
        for k in range(views * row_count):
            feat[k, spot, :] = block[k * cols : (k + 1) * cols]

    own = me * cols + lax.broadcasted_iota(jnp.int32, (cols, 1), 0)
    for k in range(views * row_count):
        view, line = k // row_count, k % row_count
        query = feat[k, pl.ds(pl.multiple_of(me * cols, 32), cols), :] * jnp.bfloat16(1.0 / 16)
        position = (count * cols - 1 - own if view else own).astype(jnp.float32)
        other = (views - 1 - view) * row_count + line
        motion[view, line] = motion_of(
            view, query, feat[other], disparity[:cols, k : k + 1], position, pool, pool_last, weights, scale_bias
        ).astype(jnp.bfloat16)
        if line == row_count - 1:
            each(halos[1][view], start, 1)

    slot = lax.broadcasted_iota(jnp.int32, (EDGE, units), 0)

    def widen(turn, view, source):
        for line in range(row_count + 2):
            if line == 0:
                centre = rows_in[turn, 0, view]
            elif line == row_count + 1:
                centre = rows_in[turn, 1, view]
            else:
                centre = source[view, line - 1]
            left = sides_in[turn, 0, view, line].astype(jnp.float32)
            right = sides_in[turn, 1, view, line].astype(jnp.float32)
            edge = jnp.where(slot == EDGE - 1, left, right)
            ring = jnp.concatenate([centre.astype(jnp.float32), edge], axis=0)
            before = pltpu.roll(ring, 1, axis=0)[:cols]
            after = pltpu.roll(ring, cols + EDGE - 1, axis=0)[:cols]
            wide[turn, view, line, :, 0:units] = before.astype(jnp.bfloat16)
            wide[turn, view, line, :, units : 2 * units] = centre
            wide[turn, view, line, :, 2 * units :] = after.astype(jnp.bfloat16)

    def convolve(turn, view, kernel, part):
        total = None
        order = (2, 1, 0) if view else (0, 1, 2)
        for a in range(3):
            window = wide[turn, view, a : a + row_count].reshape(row_count * cols, 3 * units)
            taps = jnp.concatenate([kernel[a, b, part * units : (part + 1) * units, :] for b in order], axis=0)
            term = dot(window, taps)
            total = term if total is None else total + term
        return total

    def flat_rows(values):
        return values.reshape(row_count * cols, values.shape[-1]).astype(jnp.float32)

    loads["hidden"].wait()
    loads["gate"].wait()
    gate_terms = []
    for view in range(views):
        each(halos[0][view], wait_recv, -1)
        widen(0, view, hidden_ref)
        gate_terms.append(convolve(0, view, gate, 0))
    loads["context"].wait()
    opened = []
    for view in range(views):
        each(halos[1][view], wait_recv, -1)
        widen(1, view, motion)
        terms = gate_terms[view] + convolve(1, view, gate, 1)
        gates = sigmoid(terms + flat_rows(context[view, :, :, 0 : 2 * units]))
        opened.append(gates[:, :units])
        kept = (gates[:, units:] * flat_rows(hidden_ref[view])).astype(jnp.bfloat16)
        reset[view] = kept.reshape(row_count, cols, units)
        each(halos[2][view], start, 1)
    loads["cand"].wait()
    loads["head"].wait()
    cand_terms = [convolve(1, view, cand, 1) for view in range(views)]
    for view in range(views):
        each(halos[2][view], wait_recv, -1)
        widen(2, view, reset)
        terms = cand_terms[view] + convolve(2, view, cand, 0)
        candidate = jnp.tanh(terms + flat_rows(context[view, :, :, 2 * units :]))
        state = flat_rows(hidden_ref[view])
        updated = ((1.0 - opened[view]) * state + opened[view] * candidate).astype(jnp.bfloat16)
        out_ref[view] = updated.reshape(row_count, cols, units)
        for line in range(row_count):
            step_ref[view, line : line + 1, :] = lax.dot_general(
                head_ref[...], updated[line * cols : (line + 1) * cols], (((1,), (1,)), ((), ())),
                preferred_element_type=jnp.float32,
            )
    for gather in gathers:
        gather.wait_send()
    for turn in halos:
        for copies in turn:
            each(copies, wait_send, 1)


def local(
    voxels, disparity, hidden, context, embed_first, embed_bias, embed_second, motion_weight, motion_scale,
    motion_bias, gate_kernel, candidate_kernel, head_weight,
):
    views, bins, row_count, cols = voxels.shape
    units = hidden.shape[-1]
    channels = embed_second.shape[0]
    count = lax.axis_size("col")
    pixels = views * row_count * cols
    vmem = pl.BlockSpec(memory_space=pltpu.VMEM)
    operands = (
        voxels, disparity, hidden, context, embed_first, embed_bias[None], embed_second, motion_weight,
        motion_scale[None], motion_bias[None], gate_kernel, candidate_kernel, head_weight[None],
    )
    return pl.pallas_call(
        update_kernel,
        out_shape=(
            jax.ShapeDtypeStruct(hidden.shape, jnp.bfloat16),
            jax.ShapeDtypeStruct(disparity.shape, jnp.float32),
        ),
        in_specs=[pl.BlockSpec(memory_space=pltpu.HBM)] * len(operands),
        out_specs=(vmem, vmem),
        scratch_shapes=[pltpu.VMEM(operand.shape, operand.dtype) for operand in operands]
        + [
            pltpu.VMEM((32, pixels), jnp.bfloat16),
            pltpu.VMEM((count - 1, 32, pixels), jnp.bfloat16),
            pltpu.VMEM((16, channels), jnp.float32),
            pltpu.VMEM((views * row_count, count * cols, channels), jnp.bfloat16),
            pltpu.VMEM((64, units), jnp.float32),
            pltpu.VMEM((8, 256), jnp.float32),
            pltpu.VMEM(hidden.shape, jnp.bfloat16),
            pltpu.VMEM(hidden.shape, jnp.bfloat16),
            pltpu.VMEM((3, 2, views, cols, units), jnp.bfloat16),
            pltpu.VMEM((3, 2, views, row_count + 2, EDGE, units), jnp.bfloat16),
            pltpu.VMEM((3, views, row_count + 2, cols, 3 * units), jnp.bfloat16),
            pltpu.SemaphoreType.DMA((len(operands),)),
            pltpu.SemaphoreType.DMA((count - 1,)),
            pltpu.SemaphoreType.DMA((count - 1,)),
            pltpu.SemaphoreType.DMA((3, views, 8)),
            pltpu.SemaphoreType.DMA((3, views, 8)),
        ],
        compiler_params=pltpu.CompilerParams(
            collective_id=0, has_side_effects=True, vmem_limit_bytes=64 * 2**20
        ),
    )(*operands)


def solution(mesh):
    tile = P(None, ("pair", "row"), "col")
    in_specs = (P(None, None, ("pair", "row"), "col"),) + (tile,) * 3 + (P(),) * 9
    return jax.shard_map(local, mesh=mesh, in_specs=in_specs, out_specs=(tile, tile), check_vma=False)
```

```python
import functools

import jax
import jax.numpy as jnp
from jax import lax
from jax.experimental import pallas as pl
from jax.experimental.pallas import tpu as pltpu
from jax.sharding import PartitionSpec as P

LEVELS = 4
RADIUS = 4
TAPS = 2 * RADIUS + 1
MAXDISP = 192


def pooling(length):
    row = lax.broadcasted_iota(jnp.int32, (length, length), 0)
    column = lax.broadcasted_iota(jnp.int32, (length, length), 1)
    table = jnp.zeros((length, length), jnp.float32)
    start = 0
    for level in range(1, LEVELS):
        entries = length >> level
        hit = ((row >> level) == column - start) & (column >= start) & (column < start + entries)
        table = jnp.where(hit, 1.0 / 2**level, table)
        start += entries
    return table.astype(jnp.bfloat16)


def split(values):
    high = values.astype(jnp.bfloat16)
    return high, (values - high.astype(jnp.float32)).astype(jnp.bfloat16)


def silu_half(half):
    return half + half * jnp.tanh(half)


def dot(left, right):
    return jnp.dot(left, right, preferred_element_type=jnp.float32)


def encode_block(packed, first, second):
    stacked = jnp.concatenate([packed, packed[:16]], axis=0)
    half = lax.dot_general(stacked, first, (((0,), (0,)), ((), ())), preferred_element_type=jnp.float32)
    return dot(silu_half(half).astype(jnp.bfloat16), second).astype(jnp.bfloat16)


def lookup_plan(view, centre, width_all):
    lane = lax.broadcasted_iota(jnp.int32, (1, 128), 1)
    upper = lane >= 64
    slot = lane & 63
    level = sum((slot >= TAPS * l).astype(jnp.int32) for l in range(1, LEVELS))
    tap = slot - TAPS * level - RADIUS + upper.astype(jnp.int32)

    def by_level(values, dtype):
        out = jnp.full((1, 128), values[0], dtype)
        for l in range(1, LEVELS):
            out = jnp.where(level >= l, jnp.asarray(values[l], dtype), out)
        return out

    factor = by_level([1.0 / 2**l for l in range(LEVELS)], jnp.float32)
    length = by_level([width_all >> l for l in range(LEVELS)], jnp.int32)
    group = by_level([1 << 20, 128, 64, 32], jnp.int32)
    offset = by_level([0, width_all, width_all + 128, width_all + 192], jnp.int32)
    shrink = by_level([0, 0, 64, 96], jnp.int32)
    spot = centre * factor
    floor_value = jnp.floor(spot)
    weight = spot - floor_value
    weight = jnp.where(upper, weight, 1.0 - weight)
    index = floor_value.astype(jnp.int32) + tap
    inside = (index >= 0) & (index < length) & (slot < LEVELS * TAPS)
    weight = jnp.where(inside, weight, 0.0)
    index = jnp.minimum(jnp.maximum(index, 0), length - 1)
    if view:
        index = length - 1 - index
    block = (index >= group).astype(jnp.int32) + (index >= 2 * group).astype(jnp.int32)
    place = offset + index - block * jnp.where(level > 0, group, 0) + 256 * block
    place = place - jnp.where(block == 2, shrink, 0)
    return place, weight


def motion_of(view, query, match, disparity, position, pool, pool_last, weights, scale_bias):
    width_all = match.shape[0]
    scores = lax.dot_general(query, match, (((1,), (1,)), ((), ())), preferred_element_type=jnp.float32)
    rounded = scores.astype(jnp.bfloat16)
    pieces = [scores[:, at : at + 128] for at in range(0, width_all, 128)]
    for at in range(0, width_all - 255, 256):
        pooled = dot(rounded[:, at : at + 256], pool)
        pieces += [pooled[:, :128], pooled[:, 128:]]
    pieces.append(dot(rounded[:, width_all - 128 :], pool_last))
    place, weight = lookup_plan(view, position - disparity, width_all)
    lane = place & 127
    block = place >> 7
    taken = jnp.zeros_like(weight)
    for at, piece in enumerate(pieces):
        values = jnp.take_along_axis(piece, lane, axis=1, mode="promise_in_bounds")
        taken = jnp.where(block == at, values, taken)
    taken = taken * weight
    high = taken.astype(jnp.bfloat16)
    low = (taken - high.astype(jnp.float32)).astype(jnp.bfloat16)
    both = dot(jnp.concatenate([high, low], axis=1), weights)
    half = both[:, :128] + both[:, 128:] + disparity * scale_bias[0:1] + scale_bias[1:2]
    return silu_half(half)


DIRECTIONS = ((-1, 0), (1, 0), (0, -1), (0, 1), (-1, -1), (-1, 1), (1, -1), (1, 1))
EDGE = 16


def sigmoid(values):
    return 0.5 + 0.5 * jnp.tanh(0.5 * values)


def update_kernel(
    voxels_hbm, disparity_hbm, hidden_hbm, context_hbm, first_hbm, bias_hbm, second_hbm, weight_hbm, scale_hbm,
    shift_hbm, gate_hbm, cand_hbm, head_hbm,
    out_hbm, step_hbm,
    voxels_ref, disparity_ref, hidden_ref, context, first_ref, bias_ref, second_ref, weight_ref, scale_ref,
    shift_ref, gate, cand, head_ref,
    packed, arrived, first16, feat, weight64, disp8,
    motion, reset, rows_in, sides_in, wide, blank, out_ref, step_ref,
    local_sem, out_sem, gather_send, gather_recv, halo_send, halo_recv,
):
    views, bins, row_count, cols = voxels_ref.shape
    units = hidden_ref.shape[-1]
    count, bands = lax.axis_size("col"), lax.axis_size("row")
    me, band = lax.axis_index("col"), lax.axis_index("row")

    pairs = {
        "voxels": (voxels_hbm, voxels_ref), "first": (first_hbm, first_ref), "bias": (bias_hbm, bias_ref),
        "second": (second_hbm, second_ref), "weight": (weight_hbm, weight_ref), "scale": (scale_hbm, scale_ref),
        "shift": (shift_hbm, shift_ref), "disparity": (disparity_hbm, disparity_ref),
        "hidden": (hidden_hbm, hidden_ref), "gate": (gate_hbm, gate), "context": (context_hbm, context),
        "cand": (cand_hbm, cand), "head": (head_hbm, head_ref),
    }
    loads = {
        name: pltpu.make_async_copy(source, target, local_sem.at[at])
        for at, (name, (source, target)) in enumerate(pairs.items())
    }
    loads["voxels"].start()

    def inside(dy, dx):
        row, col = band + dy, me + dx
        return (row >= 0) & (row < bands) & (col >= 0) & (col < count)

    barrier = pltpu.get_barrier_semaphore()
    expected = jnp.int32(count - 1)
    for d in range(1, count):
        pl.semaphore_signal(
            barrier, inc=1, device_id={"row": band, "col": lax.rem(me + d, count)}, device_id_type=pl.DeviceIdType.MESH
        )
    for dy, dx in DIRECTIONS:
        if dy:
            there = inside(dy, dx)
            expected = expected + there.astype(jnp.int32)

            @pl.when(there)
            def _(dy=dy, dx=dx):
                pl.semaphore_signal(
                    barrier, inc=1, device_id={"row": band + dy, "col": me + dx}, device_id_type=pl.DeviceIdType.MESH
                )

    for name in list(pairs)[1:]:
        loads[name].start()
    loads["voxels"].wait()

    pieces = [voxels_ref[k // row_count, :, k % row_count, :] for k in range(views * row_count)]
    flat = jnp.concatenate([jnp.concatenate(pieces, axis=1), jnp.ones((16 - bins, 4 * cols), jnp.float32)], axis=0)
    high, low = split(flat)
    packed[...] = jnp.concatenate([high, low], axis=0)

    blank[...] = jnp.zeros_like(blank)
    sources = (hidden_hbm, motion, reset)
    parts = [(0, slice(None))] + [(turn, view) for turn in (1, 2) for view in range(views)]

    def ends(turn, view, q, source):
        dy, dx = DIRECTIONS[q]
        line = 0 if dy < 0 else row_count - 1
        span = pl.ds(0 if dx < 0 else cols - EDGE, EDGE)
        side = 1 if dx < 0 else 0
        if dx == 0:
            return source.at[view, line], rows_in.at[turn, 1 if dy < 0 else 0, view]
        if dy == 0:
            return source.at[view, :, span], sides_in.at[turn, side, view, pl.ds(1, row_count)]
        return source.at[view, line, span], sides_in.at[turn, side, view, row_count + 1 if dy < 0 else 0]

    def place(turn, view):
        return (turn, view) if turn else (0, 0)

    for q, (dy, dx) in enumerate(DIRECTIONS):

        @pl.when(jnp.logical_not(inside(-dy, -dx)))
        def _(q=q):
            for turn, view in parts:
                src, dst = ends(turn, view, q, blank)
                pltpu.make_async_copy(src, dst, halo_recv.at[*place(turn, view), q]).start()

    pl.semaphore_wait(barrier, expected)

    gathers = [
        pltpu.make_async_remote_copy(
            src_ref=packed, dst_ref=arrived.at[s - 1], send_sem=gather_send.at[s - 1], recv_sem=gather_recv.at[s - 1],
            device_id={"row": band, "col": lax.rem(me + count - s, count)}, device_id_type=pl.DeviceIdType.MESH,
        )
        for s in range(1, count)
    ]
    for gather in gathers:
        gather.start()

    def halo(turn, view):
        copies = []
        for q, (dy, dx) in enumerate(DIRECTIONS):
            src, dst = ends(turn, view, q, sources[turn])
            copies.append(
                pltpu.make_async_remote_copy(
                    src_ref=src, dst_ref=dst, send_sem=halo_send.at[*place(turn, view), q],
                    recv_sem=halo_recv.at[*place(turn, view), q],
                    device_id={"row": band + dy, "col": me + dx}, device_id_type=pl.DeviceIdType.MESH,
                )
            )
        return copies

    halos = {part: halo(*part) for part in ((turn, 0 if turn == 0 else view) for turn, view in parts) if part[0]}
    halos[0, 0] = halo(0, slice(None))

    def start(part):
        for copy, (dy, dx) in zip(halos[part], DIRECTIONS):
            pl.when(inside(dy, dx))(copy.start)

    def arrive(part):
        for copy in halos[part]:
            copy.wait_recv()

    start((0, 0))

    for name in ("first", "bias", "second", "weight", "scale", "shift", "disparity"):
        loads[name].wait()
    first16[0:bins] = first_ref[...] * 0.5
    first16[bins : bins + 1] = bias_ref[...] * 0.5
    first_high, first_low = split(first16[...])
    first = jnp.concatenate([first_high, first_high, first_low], axis=0)
    weight64[...] = jnp.zeros_like(weight64)
    weight64[0 : LEVELS * TAPS] = weight_ref[...] * 0.5
    high, low = split(weight64[...])
    blank = jnp.zeros_like(low)
    weights = jnp.concatenate(
        [jnp.concatenate([high, low], axis=1)] * 2 + [jnp.concatenate([high, blank], axis=1)] * 2, axis=0
    )
    scale_bias = jnp.concatenate([scale_ref[...] * (0.5 / MAXDISP), shift_ref[...] * 0.5], axis=0)
    disp8[...] = jnp.zeros_like(disp8)
    for k in range(views * row_count):
        disp8[k : k + 1, 0:cols] = disparity_ref[k // row_count, k % row_count : k % row_count + 1, :]
    disparity = disp8[...].T
    pool, pool_last = pooling(256), pooling(128)

    for s in range(count):
        if s:
            gathers[s - 1].wait_recv()
        block = encode_block(arrived[s - 1] if s else packed[...], first, second_ref[...])
        spot = pl.ds(pl.multiple_of(lax.rem(me + s, count) * cols, 32), cols)
        for k in range(views * row_count):
            feat[k, spot, :] = block[k * cols : (k + 1) * cols]

    own = me * cols + lax.broadcasted_iota(jnp.int32, (cols, 1), 0)
    for k in range(views * row_count):
        view, line = k // row_count, k % row_count
        query = feat[k, pl.ds(pl.multiple_of(me * cols, 32), cols), :] * jnp.bfloat16(1.0 / 16)
        position = (count * cols - 1 - own if view else own).astype(jnp.float32)
        other = (views - 1 - view) * row_count + line
        motion[view, line] = motion_of(
            view, query, feat[other], disparity[:cols, k : k + 1], position, pool, pool_last, weights, scale_bias
        ).astype(jnp.bfloat16)
        if line == row_count - 1:
            start((1, view))

    slot = lax.broadcasted_iota(jnp.int32, (EDGE, units), 0)

    def widen(turn, view, source):
        for line in range(row_count + 2):
            if line == 0:
                centre = rows_in[turn, 0, view]
            elif line == row_count + 1:
                centre = rows_in[turn, 1, view]
            else:
                centre = source[view, line - 1]
            left = sides_in[turn, 0, view, line].astype(jnp.float32)
            right = sides_in[turn, 1, view, line].astype(jnp.float32)
            edge = jnp.where(slot == EDGE - 1, left, right)
            ring = jnp.concatenate([centre.astype(jnp.float32), edge], axis=0)
            before = pltpu.roll(ring, 1, axis=0)[:cols]
            after = pltpu.roll(ring, cols + EDGE - 1, axis=0)[:cols]
            if view:
                before, after = after, before
            wide[turn, view, line, :, 0:units] = before.astype(jnp.bfloat16)
            wide[turn, view, line, :, units : 2 * units] = centre
            wide[turn, view, line, :, 2 * units :] = after.astype(jnp.bfloat16)

    def convolve(turn, first_view, kernel, part, many=1):
        window = jnp.concatenate(
            [
                wide[turn, first_view : first_view + many, a : a + row_count].reshape(-1, 3 * units)
                for a in range(3)
            ],
            axis=1,
        )
        taps = jnp.concatenate(
            [kernel[a, b, part * units : (part + 1) * units, :] for a in range(3) for b in range(3)], axis=0
        )
        return dot(window, taps)

    def flat_rows(values):
        return values.reshape(row_count * cols, values.shape[-1]).astype(jnp.float32)

    loads["hidden"].wait()
    loads["gate"].wait()
    arrive((0, 0))
    for view in range(views):
        widen(0, view, hidden_ref)
    gate_terms = convolve(0, 0, gate, 0, views).reshape(views, row_count * cols, 2 * units)
    loads["context"].wait()
    opened = []
    for view in range(views):
        arrive((1, view))
        widen(1, view, motion)
        terms = gate_terms[view] + convolve(1, view, gate, 1)
        gates = sigmoid(terms + flat_rows(context[view, :, :, 0 : 2 * units]))
        opened.append(gates[:, :units])
        kept = (gates[:, units:] * flat_rows(hidden_ref[view])).astype(jnp.bfloat16)
        reset[view] = kept.reshape(row_count, cols, units)
        start((2, view))
    loads["cand"].wait()
    loads["head"].wait()
    cand_terms = convolve(1, 0, cand, 1, views).reshape(views, row_count * cols, units)
    exits = [pltpu.make_async_copy(out_ref.at[view], out_hbm.at[view], out_sem.at[view]) for view in range(views)]
    exits.append(pltpu.make_async_copy(step_ref, step_hbm, out_sem.at[views]))
    for view in range(views):
        arrive((2, view))
        widen(2, view, reset)
        terms = cand_terms[view] + convolve(2, view, cand, 0)
        candidate = jnp.tanh(terms + flat_rows(context[view, :, :, 2 * units :]))
        state = flat_rows(hidden_ref[view])
        updated = ((1.0 - opened[view]) * state + opened[view] * candidate).astype(jnp.bfloat16)
        out_ref[view] = updated.reshape(row_count, cols, units)
        for line in range(row_count):
            step_ref[view, line : line + 1, :] = lax.dot_general(
                head_ref[...], updated[line * cols : (line + 1) * cols], (((1,), (1,)), ((), ())),
                preferred_element_type=jnp.float32,
            )
        exits[view].start()
    exits[views].start()
    for gather in gathers:
        gather.wait_send()
    for q, (dy, dx) in enumerate(DIRECTIONS):

        @pl.when(inside(dy, dx))
        def _(q=q):
            for copies in halos.values():
                copies[q].wait_send()

    for leave in exits:
        leave.wait()


def hand_out(state_in, step_in, state_out, step_out, sem):
    copies = [
        pltpu.make_async_copy(state_in, state_out, sem.at[0]),
        pltpu.make_async_copy(step_in, step_out, sem.at[1]),
    ]
    for copy in copies:
        copy.start()
    for copy in copies:
        copy.wait()


def local(
    voxels, disparity, hidden, context, embed_first, embed_bias, embed_second, motion_weight, motion_scale,
    motion_bias, gate_kernel, candidate_kernel, head_weight,
):
    views, bins, row_count, cols = voxels.shape
    units = hidden.shape[-1]
    channels = embed_second.shape[0]
    count = lax.axis_size("col")
    pixels = views * row_count * cols
    hbm = pl.BlockSpec(memory_space=pltpu.HBM)
    operands = (
        voxels, disparity, hidden, context, embed_first, embed_bias[None], embed_second, motion_weight,
        motion_scale[None], motion_bias[None], gate_kernel, candidate_kernel, head_weight[None],
    )
    shapes = (
        jax.ShapeDtypeStruct(hidden.shape, jnp.bfloat16),
        jax.ShapeDtypeStruct(disparity.shape, jnp.float32),
    )
    results = pl.pallas_call(
        update_kernel,
        out_shape=shapes,
        in_specs=[hbm] * len(operands),
        out_specs=(hbm, hbm),
        scratch_shapes=[pltpu.VMEM(operand.shape, operand.dtype) for operand in operands]
        + [
            pltpu.VMEM((32, pixels), jnp.bfloat16),
            pltpu.VMEM((count - 1, 32, pixels), jnp.bfloat16),
            pltpu.VMEM((16, channels), jnp.float32),
            pltpu.VMEM((views * row_count, count * cols, channels), jnp.bfloat16),
            pltpu.VMEM((64, units), jnp.float32),
            pltpu.VMEM((8, 256), jnp.float32),
            pltpu.VMEM(hidden.shape, jnp.bfloat16),
            pltpu.VMEM(hidden.shape, jnp.bfloat16),
            pltpu.VMEM((3, 2, views, cols, units), jnp.bfloat16),
            pltpu.VMEM((3, 2, views, row_count + 2, EDGE, units), jnp.bfloat16),
            pltpu.VMEM((3, views, row_count + 2, cols, 3 * units), jnp.bfloat16),
            pltpu.VMEM(hidden.shape, jnp.bfloat16),
            pltpu.VMEM(hidden.shape, jnp.bfloat16),
            pltpu.VMEM(disparity.shape, jnp.float32),
            pltpu.SemaphoreType.DMA((len(operands),)),
            pltpu.SemaphoreType.DMA((views + 1,)),
            pltpu.SemaphoreType.DMA((count - 1,)),
            pltpu.SemaphoreType.DMA((count - 1,)),
            pltpu.SemaphoreType.DMA((3, views, 8)),
            pltpu.SemaphoreType.DMA((3, views, 8)),
        ],
        compiler_params=pltpu.CompilerParams(
            collective_id=0, has_side_effects=True, vmem_limit_bytes=64 * 2**20
        ),
    )(*operands)
    return pl.pallas_call(
        hand_out,
        out_shape=shapes,
        in_specs=[hbm] * 2,
        out_specs=(hbm, hbm),
        scratch_shapes=[pltpu.SemaphoreType.DMA((2,))],
        compiler_params=pltpu.CompilerParams(vmem_limit_bytes=64 * 2**20),
    )(*results)


def solution(mesh):
    tile = P(None, ("pair", "row"), "col")
    in_specs = (P(None, None, ("pair", "row"), "col"),) + (tile,) * 3 + (P(),) * 9
    return jax.shard_map(local, mesh=mesh, in_specs=in_specs, out_specs=(tile, tile), check_vma=False)
```

```python
import functools

import jax
import jax.numpy as jnp
from jax import lax
from jax.experimental import pallas as pl
from jax.experimental.pallas import tpu as pltpu
from jax.sharding import PartitionSpec as P

LEVELS = 4
RADIUS = 4
TAPS = 2 * RADIUS + 1
MAXDISP = 192


def pooling(length):
    row = lax.broadcasted_iota(jnp.int32, (length, length), 0)
    column = lax.broadcasted_iota(jnp.int32, (length, length), 1)
    table = jnp.zeros((length, length), jnp.float32)
    start = 0
    for level in range(1, LEVELS):
        entries = length >> level
        hit = ((row >> level) == column - start) & (column >= start) & (column < start + entries)
        table = jnp.where(hit, 1.0 / 2**level, table)
        start += entries
    return table.astype(jnp.bfloat16)


def split(values):
    high = values.astype(jnp.bfloat16)
    return high, (values - high.astype(jnp.float32)).astype(jnp.bfloat16)


def silu_half(half):
    return half + half * jnp.tanh(half)


def dot(left, right):
    return jnp.dot(left, right, preferred_element_type=jnp.float32)


def encode_block(packed, first, second):
    stacked = jnp.concatenate([packed, packed[:16]], axis=0)
    half = lax.dot_general(stacked, first, (((0,), (0,)), ((), ())), preferred_element_type=jnp.float32)
    return dot(silu_half(half).astype(jnp.bfloat16), second).astype(jnp.bfloat16)


def lookup_plan(view, centre, width_all):
    lane = lax.broadcasted_iota(jnp.int32, (1, 128), 1)
    upper = lane >= 64
    slot = lane & 63
    level = sum((slot >= TAPS * l).astype(jnp.int32) for l in range(1, LEVELS))
    tap = slot - TAPS * level - RADIUS + upper.astype(jnp.int32)

    def by_level(values, dtype):
        out = jnp.full((1, 128), values[0], dtype)
        for l in range(1, LEVELS):
            out = jnp.where(level >= l, jnp.asarray(values[l], dtype), out)
        return out

    factor = by_level([1.0 / 2**l for l in range(LEVELS)], jnp.float32)
    length = by_level([width_all >> l for l in range(LEVELS)], jnp.int32)
    group = by_level([1 << 20, 128, 64, 32], jnp.int32)
    offset = by_level([0, width_all, width_all + 128, width_all + 192], jnp.int32)
    shrink = by_level([0, 0, 64, 96], jnp.int32)
    spot = centre * factor
    floor_value = jnp.floor(spot)
    weight = spot - floor_value
    weight = jnp.where(upper, weight, 1.0 - weight)
    index = floor_value.astype(jnp.int32) + tap
    inside = (index >= 0) & (index < length) & (slot < LEVELS * TAPS)
    weight = jnp.where(inside, weight, 0.0)
    index = jnp.minimum(jnp.maximum(index, 0), length - 1)
    if view:
        index = length - 1 - index
    block = (index >= group).astype(jnp.int32) + (index >= 2 * group).astype(jnp.int32)
    place = offset + index - block * jnp.where(level > 0, group, 0) + 256 * block
    place = place - jnp.where(block == 2, shrink, 0)
    return place, weight


def motion_of(view, query, match, disparity, position, pool, pool_last, weights, scale_bias):
    width_all = match.shape[0]
    scores = lax.dot_general(query, match, (((1,), (1,)), ((), ())), preferred_element_type=jnp.float32)
    rounded = scores.astype(jnp.bfloat16)
    pieces = [scores[:, at : at + 128] for at in range(0, width_all, 128)]
    for at in range(0, width_all - 255, 256):
        pooled = dot(rounded[:, at : at + 256], pool)
        pieces += [pooled[:, :128], pooled[:, 128:]]
    pieces.append(dot(rounded[:, width_all - 128 :], pool_last))
    place, weight = lookup_plan(view, position - disparity, width_all)
    lane = place & 127
    block = place >> 7
    taken = jnp.zeros_like(weight)
    for at, piece in enumerate(pieces):
        values = jnp.take_along_axis(piece, lane, axis=1, mode="promise_in_bounds")
        taken = jnp.where(block == at, values, taken)
    taken = taken * weight
    high = taken.astype(jnp.bfloat16)
    low = (taken - high.astype(jnp.float32)).astype(jnp.bfloat16)
    both = dot(jnp.concatenate([high, low], axis=1), weights)
    half = both[:, :128] + both[:, 128:] + disparity * scale_bias[0:1] + scale_bias[1:2]
    return silu_half(half)


DIRECTIONS = ((-1, 0), (1, 0), (0, -1), (0, 1), (-1, -1), (-1, 1), (1, -1), (1, 1))
EDGE = 16


def sigmoid(values):
    return 0.5 + 0.5 * jnp.tanh(0.5 * values)


def update_kernel(
    voxels_hbm, disparity_hbm, hidden_hbm, context_hbm, first_hbm, bias_hbm, second_hbm, weight_hbm, scale_hbm,
    shift_hbm, gate_hbm, cand_hbm, head_hbm,
    out_hbm, step_hbm,
    voxels_ref, disparity_ref, hidden_ref, context, first_ref, bias_ref, second_ref, weight_ref, scale_ref,
    shift_ref, gate, cand, head_ref,
    packed, arrived, first16, feat, weight64, disp8,
    motion, reset, rows_in, sides_in, wide, blank, out_ref, step_ref,
    local_sem, out_sem, gather_send, gather_recv, halo_send, halo_recv,
):
    views, bins, row_count, cols = voxels_ref.shape
    units = hidden_ref.shape[-1]
    count, bands = lax.axis_size("col"), lax.axis_size("row")
    me, band = lax.axis_index("col"), lax.axis_index("row")

    pairs = {
        "voxels": (voxels_hbm, voxels_ref), "first": (first_hbm, first_ref), "bias": (bias_hbm, bias_ref),
        "second": (second_hbm, second_ref), "weight": (weight_hbm, weight_ref), "scale": (scale_hbm, scale_ref),
        "shift": (shift_hbm, shift_ref), "disparity": (disparity_hbm, disparity_ref),
        "hidden": (hidden_hbm, hidden_ref), "gate": (gate_hbm, gate), "context": (context_hbm, context),
        "cand": (cand_hbm, cand), "head": (head_hbm, head_ref),
    }
    loads = {
        name: pltpu.make_async_copy(source, target, local_sem.at[at])
        for at, (name, (source, target)) in enumerate(pairs.items())
    }
    loads["voxels"].start()

    def inside(dy, dx):
        row, col = band + dy, me + dx
        return (row >= 0) & (row < bands) & (col >= 0) & (col < count)

    barrier = pltpu.get_barrier_semaphore()
    expected = jnp.int32(count - 1)
    for d in range(1, count):
        pl.semaphore_signal(
            barrier, inc=1, device_id={"row": band, "col": lax.rem(me + d, count)}, device_id_type=pl.DeviceIdType.MESH
        )
    for dy, dx in DIRECTIONS:
        if dy:
            there = inside(dy, dx)
            expected = expected + there.astype(jnp.int32)

            @pl.when(there)
            def _(dy=dy, dx=dx):
                pl.semaphore_signal(
                    barrier, inc=1, device_id={"row": band + dy, "col": me + dx}, device_id_type=pl.DeviceIdType.MESH
                )

    for name in list(pairs)[1:]:
        loads[name].start()
    loads["voxels"].wait()

    pieces = [voxels_ref[k // row_count, :, k % row_count, :] for k in range(views * row_count)]
    flat = jnp.concatenate([jnp.concatenate(pieces, axis=1), jnp.ones((16 - bins, 4 * cols), jnp.float32)], axis=0)
    high, low = split(flat)
    packed[...] = jnp.concatenate([high, low], axis=0)

    blank[...] = jnp.zeros_like(blank)
    sources = (hidden_hbm, motion, reset)
    parts = [(0, slice(None))] + [(turn, view) for turn in (1, 2) for view in range(views)]

    def ends(turn, view, q, source):
        dy, dx = DIRECTIONS[q]
        line = 0 if dy < 0 else row_count - 1
        span = pl.ds(0 if dx < 0 else cols - EDGE, EDGE)
        side = 1 if dx < 0 else 0
        if dx == 0:
            return source.at[view, line], rows_in.at[turn, 1 if dy < 0 else 0, view]
        if dy == 0:
            return source.at[view, :, span], sides_in.at[turn, side, view, pl.ds(1, row_count)]
        return source.at[view, line, span], sides_in.at[turn, side, view, row_count + 1 if dy < 0 else 0]

    def place(turn, view):
        return (turn, view) if turn else (0, 0)

    for q, (dy, dx) in enumerate(DIRECTIONS):

        @pl.when(jnp.logical_not(inside(-dy, -dx)))
        def _(q=q):
            for turn, view in parts:
                src, dst = ends(turn, view, q, blank)
                pltpu.make_async_copy(src, dst, halo_recv.at[*place(turn, view), q]).start()

    pl.semaphore_wait(barrier, expected)

    gathers = [
        pltpu.make_async_remote_copy(
            src_ref=packed, dst_ref=arrived.at[s - 1], send_sem=gather_send.at[s - 1], recv_sem=gather_recv.at[s - 1],
            device_id={"row": band, "col": lax.rem(me + count - s, count)}, device_id_type=pl.DeviceIdType.MESH,
        )
        for s in range(1, count)
    ]
    for gather in gathers:
        gather.start()

    def halo(turn, view):
        copies = []
        for q, (dy, dx) in enumerate(DIRECTIONS):
            src, dst = ends(turn, view, q, sources[turn])
            copies.append(
                pltpu.make_async_remote_copy(
                    src_ref=src, dst_ref=dst, send_sem=halo_send.at[*place(turn, view), q],
                    recv_sem=halo_recv.at[*place(turn, view), q],
                    device_id={"row": band + dy, "col": me + dx}, device_id_type=pl.DeviceIdType.MESH,
                )
            )
        return copies

    halos = {part: halo(*part) for part in ((turn, 0 if turn == 0 else view) for turn, view in parts) if part[0]}
    halos[0, 0] = halo(0, slice(None))

    def start(part):
        for copy, (dy, dx) in zip(halos[part], DIRECTIONS):
            pl.when(inside(dy, dx))(copy.start)

    def arrive(part):
        for copy in halos[part]:
            copy.wait_recv()

    start((0, 0))

    for name in ("first", "bias", "second", "weight", "scale", "shift", "disparity"):
        loads[name].wait()
    first16[0:bins] = first_ref[...] * 0.5
    first16[bins : bins + 1] = bias_ref[...] * 0.5
    first_high, first_low = split(first16[...])
    first = jnp.concatenate([first_high, first_high, first_low], axis=0)
    weight64[...] = jnp.zeros_like(weight64)
    weight64[0 : LEVELS * TAPS] = weight_ref[...] * 0.5
    high, low = split(weight64[...])
    blank = jnp.zeros_like(low)
    weights = jnp.concatenate(
        [jnp.concatenate([high, low], axis=1)] * 2 + [jnp.concatenate([high, blank], axis=1)] * 2, axis=0
    )
    scale_bias = jnp.concatenate([scale_ref[...] * (0.5 / MAXDISP), shift_ref[...] * 0.5], axis=0)
    disp8[...] = jnp.zeros_like(disp8)
    for k in range(views * row_count):
        disp8[k : k + 1, 0:cols] = disparity_ref[k // row_count, k % row_count : k % row_count + 1, :]
    disparity = disp8[...].T
    pool, pool_last = pooling(256), pooling(128)

    for s in range(count):
        if s:
            gathers[s - 1].wait_recv()
        block = encode_block(arrived[s - 1] if s else packed[...], first, second_ref[...])
        spot = pl.ds(pl.multiple_of(lax.rem(me + s, count) * cols, 32), cols)
        for k in range(views * row_count):
            feat[k, spot, :] = block[k * cols : (k + 1) * cols]

    own = me * cols + lax.broadcasted_iota(jnp.int32, (cols, 1), 0)
    for k in range(views * row_count):
        view, line = k // row_count, k % row_count
        query = feat[k, pl.ds(pl.multiple_of(me * cols, 32), cols), :] * jnp.bfloat16(1.0 / 16)
        position = (count * cols - 1 - own if view else own).astype(jnp.float32)
        other = (views - 1 - view) * row_count + line
        motion[view, line] = motion_of(
            view, query, feat[other], disparity[:cols, k : k + 1], position, pool, pool_last, weights, scale_bias
        ).astype(jnp.bfloat16)
        if line == row_count - 1:
            start((1, view))

    slot = lax.broadcasted_iota(jnp.int32, (EDGE, units), 0)

    def widen(turn, view, source):
        for line in range(row_count + 2):
            if line == 0:
                centre = rows_in[turn, 0, view]
            elif line == row_count + 1:
                centre = rows_in[turn, 1, view]
            else:
                centre = source[view, line - 1]
            left = sides_in[turn, 0, view, line].astype(jnp.float32)
            right = sides_in[turn, 1, view, line].astype(jnp.float32)
            edge = jnp.where(slot == EDGE - 1, left, right)
            ring = jnp.concatenate([centre.astype(jnp.float32), edge], axis=0)
            before = pltpu.roll(ring, 1, axis=0)[:cols]
            after = pltpu.roll(ring, cols + EDGE - 1, axis=0)[:cols]
            if view:
                before, after = after, before
            wide[turn, view, line, :, 0:units] = before.astype(jnp.bfloat16)
            wide[turn, view, line, :, units : 2 * units] = centre
            wide[turn, view, line, :, 2 * units :] = after.astype(jnp.bfloat16)

    def convolve(turn, first_view, kernel, part, channels, many=1):
        window = jnp.concatenate(
            [
                wide[turn, first_view : first_view + many, a : a + row_count].reshape(-1, 3 * units)
                for a in range(3)
            ],
            axis=1,
        )
        taps = jnp.concatenate(
            [kernel[a, b, part * units : (part + 1) * units, channels] for a in range(3) for b in range(3)], axis=0
        )
        return dot(window, taps)

    def flat_rows(values):
        return values.reshape(row_count * cols, values.shape[-1]).astype(jnp.float32)

    loads["hidden"].wait()
    loads["gate"].wait()
    arrive((0, 0))
    for view in range(views):
        widen(0, view, hidden_ref)
    early, late = slice(units, 2 * units), slice(0, units)
    reset_terms = convolve(0, 0, gate, 0, early, views).reshape(views, row_count * cols, units)
    loads["context"].wait()
    for view in range(views):
        arrive((1, view))
        widen(1, view, motion)
        terms = reset_terms[view] + convolve(1, view, gate, 1, early)
        kept = sigmoid(terms + flat_rows(context[view, :, :, early])) * flat_rows(hidden_ref[view])
        reset[view] = kept.astype(jnp.bfloat16).reshape(row_count, cols, units)
        start((2, view))
    loads["cand"].wait()
    loads["head"].wait()
    open_terms = convolve(0, 0, gate, 0, late, views) + convolve(1, 0, gate, 1, late, views)
    opened = sigmoid(open_terms.reshape(views, row_count * cols, units) + context[:, :, :, late].reshape(
        views, row_count * cols, units).astype(jnp.float32))
    cand_terms = convolve(1, 0, cand, 1, late, views).reshape(views, row_count * cols, units)
    exits = [pltpu.make_async_copy(out_ref.at[view], out_hbm.at[view], out_sem.at[view]) for view in range(views)]
    exits.append(pltpu.make_async_copy(step_ref, step_hbm, out_sem.at[views]))
    for view in range(views):
        arrive((2, view))
        widen(2, view, reset)
        terms = cand_terms[view] + convolve(2, view, cand, 0, late)
        candidate = jnp.tanh(terms + flat_rows(context[view, :, :, 2 * units :]))
        state = flat_rows(hidden_ref[view])
        updated = ((1.0 - opened[view]) * state + opened[view] * candidate).astype(jnp.bfloat16)
        out_ref[view] = updated.reshape(row_count, cols, units)
        for line in range(row_count):
            step_ref[view, line : line + 1, :] = lax.dot_general(
                head_ref[...], updated[line * cols : (line + 1) * cols], (((1,), (1,)), ((), ())),
                preferred_element_type=jnp.float32,
            )
        exits[view].start()
    exits[views].start()
    for gather in gathers:
        gather.wait_send()
    for q, (dy, dx) in enumerate(DIRECTIONS):

        @pl.when(inside(dy, dx))
        def _(q=q):
            for copies in halos.values():
                copies[q].wait_send()

    for leave in exits:
        leave.wait()


def hand_out(state_in, step_in, state_out, step_out, state, step, sem):
    views = state.shape[0]
    arrivals = [pltpu.make_async_copy(state_in.at[view], state.at[view], sem.at[0, view]) for view in range(views)]
    exits = [pltpu.make_async_copy(state.at[view], state_out.at[view], sem.at[1, view]) for view in range(views)]
    arrivals.append(pltpu.make_async_copy(step_in, step, sem.at[0, views]))
    exits.append(pltpu.make_async_copy(step, step_out, sem.at[1, views]))
    for copy in arrivals:
        copy.start()
    for arrival, leave in zip(arrivals, exits):
        arrival.wait()
        leave.start()
    for leave in exits:
        leave.wait()


def local(
    voxels, disparity, hidden, context, embed_first, embed_bias, embed_second, motion_weight, motion_scale,
    motion_bias, gate_kernel, candidate_kernel, head_weight,
):
    views, bins, row_count, cols = voxels.shape
    units = hidden.shape[-1]
    channels = embed_second.shape[0]
    count = lax.axis_size("col")
    pixels = views * row_count * cols
    hbm = pl.BlockSpec(memory_space=pltpu.HBM)
    operands = (
        voxels, disparity, hidden, context, embed_first, embed_bias[None], embed_second, motion_weight,
        motion_scale[None], motion_bias[None], gate_kernel, candidate_kernel, head_weight[None],
    )
    shapes = (
        jax.ShapeDtypeStruct(hidden.shape, jnp.bfloat16),
        jax.ShapeDtypeStruct(disparity.shape, jnp.float32),
    )
    results = pl.pallas_call(
        update_kernel,
        out_shape=shapes,
        in_specs=[hbm] * len(operands),
        out_specs=(hbm, hbm),
        scratch_shapes=[pltpu.VMEM(operand.shape, operand.dtype) for operand in operands]
        + [
            pltpu.VMEM((32, pixels), jnp.bfloat16),
            pltpu.VMEM((count - 1, 32, pixels), jnp.bfloat16),
            pltpu.VMEM((16, channels), jnp.float32),
            pltpu.VMEM((views * row_count, count * cols, channels), jnp.bfloat16),
            pltpu.VMEM((64, units), jnp.float32),
            pltpu.VMEM((8, 256), jnp.float32),
            pltpu.VMEM(hidden.shape, jnp.bfloat16),
            pltpu.VMEM(hidden.shape, jnp.bfloat16),
            pltpu.VMEM((3, 2, views, cols, units), jnp.bfloat16),
            pltpu.VMEM((3, 2, views, row_count + 2, EDGE, units), jnp.bfloat16),
            pltpu.VMEM((3, views, row_count + 2, cols, 3 * units), jnp.bfloat16),
            pltpu.VMEM(hidden.shape, jnp.bfloat16),
            pltpu.VMEM(hidden.shape, jnp.bfloat16),
            pltpu.VMEM(disparity.shape, jnp.float32),
            pltpu.SemaphoreType.DMA((len(operands),)),
            pltpu.SemaphoreType.DMA((views + 1,)),
            pltpu.SemaphoreType.DMA((count - 1,)),
            pltpu.SemaphoreType.DMA((count - 1,)),
            pltpu.SemaphoreType.DMA((3, views, 8)),
            pltpu.SemaphoreType.DMA((3, views, 8)),
        ],
        compiler_params=pltpu.CompilerParams(
            collective_id=0, has_side_effects=True, vmem_limit_bytes=64 * 2**20
        ),
    )(*operands)
    return pl.pallas_call(
        hand_out,
        out_shape=shapes,
        in_specs=[hbm] * 2,
        out_specs=(hbm, hbm),
        scratch_shapes=[
            pltpu.VMEM(hidden.shape, jnp.bfloat16),
            pltpu.VMEM(disparity.shape, jnp.float32),
            pltpu.SemaphoreType.DMA((2, views + 1)),
        ],
        compiler_params=pltpu.CompilerParams(vmem_limit_bytes=64 * 2**20),
    )(*results)


def solution(mesh):
    tile = P(None, ("pair", "row"), "col")
    in_specs = (P(None, None, ("pair", "row"), "col"),) + (tile,) * 3 + (P(),) * 9
    return jax.shard_map(local, mesh=mesh, in_specs=in_specs, out_specs=(tile, tile), check_vma=False)
```

```python
import functools

import jax
import jax.numpy as jnp
from jax import lax
from jax.experimental import pallas as pl
from jax.experimental.pallas import tpu as pltpu
from jax.sharding import PartitionSpec as P

LEVELS = 4
RADIUS = 4
TAPS = 2 * RADIUS + 1
MAXDISP = 192


def pooling(length):
    row = lax.broadcasted_iota(jnp.int32, (length, length), 0)
    column = lax.broadcasted_iota(jnp.int32, (length, length), 1)
    table = jnp.zeros((length, length), jnp.float32)
    start = 0
    for level in range(1, LEVELS):
        entries = length >> level
        hit = ((row >> level) == column - start) & (column >= start) & (column < start + entries)
        table = jnp.where(hit, 1.0 / 2**level, table)
        start += entries
    return table.astype(jnp.bfloat16)


def split(values):
    high = values.astype(jnp.bfloat16)
    return high, (values - high.astype(jnp.float32)).astype(jnp.bfloat16)


def silu_half(half):
    return half + half * jnp.tanh(half)


def dot(left, right):
    return jnp.dot(left, right, preferred_element_type=jnp.float32)


def encode_block(packed, first, second):
    stacked = jnp.concatenate([packed, packed[:16]], axis=0)
    half = lax.dot_general(stacked, first, (((0,), (0,)), ((), ())), preferred_element_type=jnp.float32)
    return dot(silu_half(half).astype(jnp.bfloat16), second).astype(jnp.bfloat16)


def lookup_plan(view, centre, width_all):
    lane = lax.broadcasted_iota(jnp.int32, (1, 128), 1)
    upper = lane >= 64
    slot = lane & 63
    level = sum((slot >= TAPS * l).astype(jnp.int32) for l in range(1, LEVELS))
    tap = slot - TAPS * level - RADIUS + upper.astype(jnp.int32)

    def by_level(values, dtype):
        out = jnp.full((1, 128), values[0], dtype)
        for l in range(1, LEVELS):
            out = jnp.where(level >= l, jnp.asarray(values[l], dtype), out)
        return out

    factor = by_level([1.0 / 2**l for l in range(LEVELS)], jnp.float32)
    length = by_level([width_all >> l for l in range(LEVELS)], jnp.int32)
    group = by_level([1 << 20, 128, 64, 32], jnp.int32)
    offset = by_level([0, width_all, width_all + 128, width_all + 192], jnp.int32)
    shrink = by_level([0, 0, 64, 96], jnp.int32)
    spot = centre * factor
    floor_value = jnp.floor(spot)
    weight = spot - floor_value
    weight = jnp.where(upper, weight, 1.0 - weight)
    index = floor_value.astype(jnp.int32) + tap
    inside = (index >= 0) & (index < length) & (slot < LEVELS * TAPS)
    weight = jnp.where(inside, weight, 0.0)
    index = jnp.minimum(jnp.maximum(index, 0), length - 1)
    if view:
        index = length - 1 - index
    block = (index >= group).astype(jnp.int32) + (index >= 2 * group).astype(jnp.int32)
    place = offset + index - block * jnp.where(level > 0, group, 0) + 256 * block
    place = place - jnp.where(block == 2, shrink, 0)
    return place, weight


def motion_of(view, query, match, disparity, position, pool, pool_last, weights, scale_bias):
    width_all = match.shape[0]
    scores = lax.dot_general(query, match, (((1,), (1,)), ((), ())), preferred_element_type=jnp.float32)
    rounded = scores.astype(jnp.bfloat16)
    pieces = [scores[:, at : at + 128] for at in range(0, width_all, 128)]
    for at in range(0, width_all - 255, 256):
        pooled = dot(rounded[:, at : at + 256], pool)
        pieces += [pooled[:, :128], pooled[:, 128:]]
    pieces.append(dot(rounded[:, width_all - 128 :], pool_last))
    place, weight = lookup_plan(view, position - disparity, width_all)
    lane = place & 127
    block = place >> 7
    taken = jnp.zeros_like(weight)
    for at, piece in enumerate(pieces):
        values = jnp.take_along_axis(piece, lane, axis=1, mode="promise_in_bounds")
        taken = jnp.where(block == at, values, taken)
    taken = taken * weight
    high = taken.astype(jnp.bfloat16)
    low = (taken - high.astype(jnp.float32)).astype(jnp.bfloat16)
    both = dot(jnp.concatenate([high, low], axis=1), weights)
    half = both[:, :128] + both[:, 128:] + disparity * scale_bias[0:1] + scale_bias[1:2]
    return silu_half(half)


DIRECTIONS = ((-1, 0), (1, 0), (0, -1), (0, 1), (-1, -1), (-1, 1), (1, -1), (1, 1))
EDGE = 16


def sigmoid(values):
    return 0.5 + 0.5 * jnp.tanh(0.5 * values)


def update_kernel(
    voxels_hbm, disparity_hbm, hidden_hbm, context_hbm, first_hbm, bias_hbm, second_hbm, weight_hbm, scale_hbm,
    shift_hbm, gate_hbm, cand_hbm, head_hbm,
    out_hbm, step_hbm,
    voxels_ref, disparity_ref, hidden_ref, context, first_ref, bias_ref, second_ref, weight_ref, scale_ref,
    shift_ref, gate, cand, head_ref,
    packed, arrived, first16, feat, weight64, disp8,
    motion, reset, rows_in, sides_in, wide, blank, out_ref, step_ref,
    local_sem, out_sem, gather_send, gather_recv, halo_send, halo_recv,
):
    views, bins, row_count, cols = voxels_ref.shape
    units = hidden_ref.shape[-1]
    count, bands = lax.axis_size("col"), lax.axis_size("row")
    me, band = lax.axis_index("col"), lax.axis_index("row")

    pairs = {
        "voxels": (voxels_hbm, voxels_ref), "first": (first_hbm, first_ref), "bias": (bias_hbm, bias_ref),
        "second": (second_hbm, second_ref), "weight": (weight_hbm, weight_ref), "scale": (scale_hbm, scale_ref),
        "shift": (shift_hbm, shift_ref), "disparity": (disparity_hbm, disparity_ref),
        "hidden": (hidden_hbm, hidden_ref), "gate": (gate_hbm, gate), "context": (context_hbm, context),
        "cand": (cand_hbm, cand), "head": (head_hbm, head_ref),
    }
    loads = {
        name: pltpu.make_async_copy(source, target, local_sem.at[at])
        for at, (name, (source, target)) in enumerate(pairs.items())
    }
    loads["voxels"].start()

    def inside(dy, dx):
        row, col = band + dy, me + dx
        return (row >= 0) & (row < bands) & (col >= 0) & (col < count)

    barrier = pltpu.get_barrier_semaphore()
    expected = jnp.int32(count - 1)
    for d in range(1, count):
        pl.semaphore_signal(
            barrier, inc=1, device_id={"row": band, "col": lax.rem(me + d, count)}, device_id_type=pl.DeviceIdType.MESH
        )
    for dy, dx in DIRECTIONS:
        if dy:
            there = inside(dy, dx)
            expected = expected + there.astype(jnp.int32)

            @pl.when(there)
            def _(dy=dy, dx=dx):
                pl.semaphore_signal(
                    barrier, inc=1, device_id={"row": band + dy, "col": me + dx}, device_id_type=pl.DeviceIdType.MESH
                )

    for name in list(pairs)[1:]:
        loads[name].start()
    loads["voxels"].wait()

    pieces = [voxels_ref[k // row_count, :, k % row_count, :] for k in range(views * row_count)]
    flat = jnp.concatenate([jnp.concatenate(pieces, axis=1), jnp.ones((16 - bins, 4 * cols), jnp.float32)], axis=0)
    high, low = split(flat)
    packed[...] = jnp.concatenate([high, low], axis=0)

    sources = (hidden_hbm, motion, reset)
    parts = [(0, slice(None))] + [(turn, view) for turn in (1, 2) for view in range(views)]

    def ends(turn, view, q, source):
        dy, dx = DIRECTIONS[q]
        line = 0 if dy < 0 else row_count - 1
        span = pl.ds(0 if dx < 0 else cols - EDGE, EDGE)
        side = 1 if dx < 0 else 0
        if dx == 0:
            return source.at[view, line], rows_in.at[turn, 1 if dy < 0 else 0, view]
        if dy == 0:
            return source.at[view, :, span], sides_in.at[turn, side, view, pl.ds(1, row_count)]
        return source.at[view, line, span], sides_in.at[turn, side, view, row_count + 1 if dy < 0 else 0]

    def place(turn, view):
        return (turn, view) if turn else (0, 0)

    pl.semaphore_wait(barrier, expected)

    gathers = [
        pltpu.make_async_remote_copy(
            src_ref=packed, dst_ref=arrived.at[s - 1], send_sem=gather_send.at[s - 1], recv_sem=gather_recv.at[s - 1],
            device_id={"row": band, "col": lax.rem(me + count - s, count)}, device_id_type=pl.DeviceIdType.MESH,
        )
        for s in range(1, count)
    ]
    for gather in gathers:
        gather.start()

    def halo(turn, view):
        copies = []
        for q, (dy, dx) in enumerate(DIRECTIONS):
            src, dst = ends(turn, view, q, sources[turn])
            copies.append(
                pltpu.make_async_remote_copy(
                    src_ref=src, dst_ref=dst, send_sem=halo_send.at[*place(turn, view), q],
                    recv_sem=halo_recv.at[*place(turn, view), q],
                    device_id={"row": band + dy, "col": me + dx}, device_id_type=pl.DeviceIdType.MESH,
                )
            )
        return copies

    halos = {part: halo(*part) for part in ((turn, 0 if turn == 0 else view) for turn, view in parts) if part[0]}
    halos[0, 0] = halo(0, slice(None))

    def start(part, ways=(-1, 0, 1)):
        for copy, (dy, dx) in zip(halos[part], DIRECTIONS):
            if dy in ways:
                pl.when(inside(dy, dx))(copy.start)

    def arrive(part):
        for copy in halos[part]:
            copy.wait_recv()

    start((0, 0))

    blank[...] = jnp.zeros_like(blank)
    for q, (dy, dx) in enumerate(DIRECTIONS):

        @pl.when(jnp.logical_not(inside(-dy, -dx)))
        def _(q=q):
            for turn, view in parts:
                src, dst = ends(turn, view, q, blank)
                pltpu.make_async_copy(src, dst, halo_recv.at[*place(turn, view), q]).start()

    for name in ("first", "bias", "second", "weight", "scale", "shift", "disparity"):
        loads[name].wait()
    first16[0:bins] = first_ref[...] * 0.5
    first16[bins : bins + 1] = bias_ref[...] * 0.5
    first_high, first_low = split(first16[...])
    first = jnp.concatenate([first_high, first_high, first_low], axis=0)
    weight64[...] = jnp.zeros_like(weight64)
    weight64[0 : LEVELS * TAPS] = weight_ref[...] * 0.5
    high, low = split(weight64[...])
    blank = jnp.zeros_like(low)
    weights = jnp.concatenate(
        [jnp.concatenate([high, low], axis=1)] * 2 + [jnp.concatenate([high, blank], axis=1)] * 2, axis=0
    )
    scale_bias = jnp.concatenate([scale_ref[...] * (0.5 / MAXDISP), shift_ref[...] * 0.5], axis=0)
    disp8[...] = jnp.zeros_like(disp8)
    for k in range(views * row_count):
        disp8[k : k + 1, 0:cols] = disparity_ref[k // row_count, k % row_count : k % row_count + 1, :]
    disparity = disp8[...].T
    pool, pool_last = pooling(256), pooling(128)

    slot = lax.broadcasted_iota(jnp.int32, (EDGE, units), 0)

    def widen(turn, view, source):
        for line in range(row_count + 2):
            if line == 0:
                centre = rows_in[turn, 0, view]
            elif line == row_count + 1:
                centre = rows_in[turn, 1, view]
            else:
                centre = source[view, line - 1]
            left = sides_in[turn, 0, view, line].astype(jnp.float32)
            right = sides_in[turn, 1, view, line].astype(jnp.float32)
            edge = jnp.where(slot == EDGE - 1, left, right)
            ring = jnp.concatenate([centre.astype(jnp.float32), edge], axis=0)
            before = pltpu.roll(ring, 1, axis=0)[:cols]
            after = pltpu.roll(ring, cols + EDGE - 1, axis=0)[:cols]
            if view:
                before, after = after, before
            wide[turn, view, line, :, 0:units] = before.astype(jnp.bfloat16)
            wide[turn, view, line, :, units : 2 * units] = centre
            wide[turn, view, line, :, 2 * units :] = after.astype(jnp.bfloat16)

    def convolve(turn, first_view, kernel, part, channels, many=1):
        window = jnp.concatenate(
            [
                wide[turn, first_view : first_view + many, a : a + row_count].reshape(-1, 3 * units)
                for a in range(3)
            ],
            axis=1,
        )
        taps = jnp.concatenate(
            [kernel[a, b, part * units : (part + 1) * units, channels] for a in range(3) for b in range(3)], axis=0
        )
        return dot(window, taps)

    def flat_rows(values):
        return values.reshape(row_count * cols, values.shape[-1]).astype(jnp.float32)

    for s in range(count):
        if s:
            gathers[s - 1].wait_recv()
        block = encode_block(arrived[s - 1] if s else packed[...], first, second_ref[...])
        spot = pl.ds(pl.multiple_of(lax.rem(me + s, count) * cols, 32), cols)
        for k in range(views * row_count):
            feat[k, spot, :] = block[k * cols : (k + 1) * cols]
        if s == 0:
            loads["hidden"].wait()
            loads["gate"].wait()
            arrive((0, 0))
            for view in range(views):
                widen(0, view, hidden_ref)
            early, late = slice(units, 2 * units), slice(0, units)
            gate_terms = convolve(0, 0, gate, 0, slice(0, 2 * units), views).reshape(views, row_count * cols, 2 * units)

    own = me * cols + lax.broadcasted_iota(jnp.int32, (cols, 1), 0)
    for k in range(views * row_count):
        view, line = k // row_count, k % row_count
        query = feat[k, pl.ds(pl.multiple_of(me * cols, 32), cols), :] * jnp.bfloat16(1.0 / 16)
        position = (count * cols - 1 - own if view else own).astype(jnp.float32)
        other = (views - 1 - view) * row_count + line
        motion[view, line] = motion_of(
            view, query, feat[other], disparity[:cols, k : k + 1], position, pool, pool_last, weights, scale_bias
        ).astype(jnp.bfloat16)
        if line == 0:
            start((1, view), (-1,))
        if line == row_count - 1:
            start((1, view), (0, 1))

    loads["context"].wait()
    for view in range(views):
        arrive((1, view))
        widen(1, view, motion)
        terms = gate_terms[view][:, early] + convolve(1, view, gate, 1, early)
        kept = sigmoid(terms + flat_rows(context[view, :, :, early])) * flat_rows(hidden_ref[view])
        reset[view] = kept.astype(jnp.bfloat16).reshape(row_count, cols, units)
        start((2, view))
    loads["cand"].wait()
    loads["head"].wait()
    open_terms = gate_terms[:, :, late] + convolve(1, 0, gate, 1, late, views).reshape(views, -1, units)
    opened = sigmoid(open_terms + context[:, :, :, late].reshape(
        views, row_count * cols, units).astype(jnp.float32))
    cand_terms = convolve(1, 0, cand, 1, late, views).reshape(views, row_count * cols, units)
    exits = [pltpu.make_async_copy(out_ref.at[view], out_hbm.at[view], out_sem.at[view]) for view in range(views)]
    exits.append(pltpu.make_async_copy(step_ref, step_hbm, out_sem.at[views]))
    for view in range(views):
        arrive((2, view))
        widen(2, view, reset)
        terms = cand_terms[view] + convolve(2, view, cand, 0, late)
        candidate = jnp.tanh(terms + flat_rows(context[view, :, :, 2 * units :]))
        state = flat_rows(hidden_ref[view])
        updated = ((1.0 - opened[view]) * state + opened[view] * candidate).astype(jnp.bfloat16)
        out_ref[view] = updated.reshape(row_count, cols, units)
        for line in range(row_count):
            step_ref[view, line : line + 1, :] = lax.dot_general(
                head_ref[...], updated[line * cols : (line + 1) * cols], (((1,), (1,)), ((), ())),
                preferred_element_type=jnp.float32,
            )
        exits[view].start()
    exits[views].start()
    for gather in gathers:
        gather.wait_send()
    for q, (dy, dx) in enumerate(DIRECTIONS):

        @pl.when(inside(dy, dx))
        def _(q=q):
            for copies in halos.values():
                copies[q].wait_send()

    for leave in exits:
        leave.wait()


def hand_out(state_in, step_in, state_out, step_out, state, step, sem):
    views = state.shape[0]
    arrivals = [pltpu.make_async_copy(state_in.at[view], state.at[view], sem.at[0, view]) for view in range(views)]
    exits = [pltpu.make_async_copy(state.at[view], state_out.at[view], sem.at[1, view]) for view in range(views)]
    arrivals.append(pltpu.make_async_copy(step_in, step, sem.at[0, views]))
    exits.append(pltpu.make_async_copy(step, step_out, sem.at[1, views]))
    for copy in arrivals:
        copy.start()
    for arrival, leave in zip(arrivals, exits):
        arrival.wait()
        leave.start()
    for leave in exits:
        leave.wait()


def local(
    voxels, disparity, hidden, context, embed_first, embed_bias, embed_second, motion_weight, motion_scale,
    motion_bias, gate_kernel, candidate_kernel, head_weight,
):
    views, bins, row_count, cols = voxels.shape
    units = hidden.shape[-1]
    channels = embed_second.shape[0]
    count = lax.axis_size("col")
    pixels = views * row_count * cols
    hbm = pl.BlockSpec(memory_space=pltpu.HBM)
    operands = (
        voxels, disparity, hidden, context, embed_first, embed_bias[None], embed_second, motion_weight,
        motion_scale[None], motion_bias[None], gate_kernel, candidate_kernel, head_weight[None],
    )
    shapes = (
        jax.ShapeDtypeStruct(hidden.shape, jnp.bfloat16),
        jax.ShapeDtypeStruct(disparity.shape, jnp.float32),
    )
    results = pl.pallas_call(
        update_kernel,
        out_shape=shapes,
        in_specs=[hbm] * len(operands),
        out_specs=(hbm, hbm),
        scratch_shapes=[pltpu.VMEM(operand.shape, operand.dtype) for operand in operands]
        + [
            pltpu.VMEM((32, pixels), jnp.bfloat16),
            pltpu.VMEM((count - 1, 32, pixels), jnp.bfloat16),
            pltpu.VMEM((16, channels), jnp.float32),
            pltpu.VMEM((views * row_count, count * cols, channels), jnp.bfloat16),
            pltpu.VMEM((64, units), jnp.float32),
            pltpu.VMEM((8, 256), jnp.float32),
            pltpu.VMEM(hidden.shape, jnp.bfloat16),
            pltpu.VMEM(hidden.shape, jnp.bfloat16),
            pltpu.VMEM((3, 2, views, cols, units), jnp.bfloat16),
            pltpu.VMEM((3, 2, views, row_count + 2, EDGE, units), jnp.bfloat16),
            pltpu.VMEM((3, views, row_count + 2, cols, 3 * units), jnp.bfloat16),
            pltpu.VMEM(hidden.shape, jnp.bfloat16),
            pltpu.VMEM(hidden.shape, jnp.bfloat16),
            pltpu.VMEM(disparity.shape, jnp.float32),
            pltpu.SemaphoreType.DMA((len(operands),)),
            pltpu.SemaphoreType.DMA((views + 1,)),
            pltpu.SemaphoreType.DMA((count - 1,)),
            pltpu.SemaphoreType.DMA((count - 1,)),
            pltpu.SemaphoreType.DMA((3, views, 8)),
            pltpu.SemaphoreType.DMA((3, views, 8)),
        ],
        compiler_params=pltpu.CompilerParams(
            collective_id=0, has_side_effects=True, vmem_limit_bytes=64 * 2**20
        ),
    )(*operands)
    return pl.pallas_call(
        hand_out,
        out_shape=shapes,
        in_specs=[hbm] * 2,
        out_specs=(hbm, hbm),
        scratch_shapes=[
            pltpu.VMEM(hidden.shape, jnp.bfloat16),
            pltpu.VMEM(disparity.shape, jnp.float32),
            pltpu.SemaphoreType.DMA((2, views + 1)),
        ],
        compiler_params=pltpu.CompilerParams(vmem_limit_bytes=64 * 2**20),
    )(*results)


def solution(mesh):
    tile = P(None, ("pair", "row"), "col")
    in_specs = (P(None, None, ("pair", "row"), "col"),) + (tile,) * 3 + (P(),) * 9
    return jax.shard_map(local, mesh=mesh, in_specs=in_specs, out_specs=(tile, tile), check_vma=False)
```

```python
import functools

import jax
import jax.numpy as jnp
from jax import lax
from jax.experimental import pallas as pl
from jax.experimental.pallas import tpu as pltpu
from jax.sharding import PartitionSpec as P

LEVELS = 4
RADIUS = 4
TAPS = 2 * RADIUS + 1
MAXDISP = 192


def pooling(length):
    row = lax.broadcasted_iota(jnp.int32, (length, length), 0)
    column = lax.broadcasted_iota(jnp.int32, (length, length), 1)
    table = jnp.zeros((length, length), jnp.float32)
    start = 0
    for level in range(1, LEVELS):
        entries = length >> level
        hit = ((row >> level) == column - start) & (column >= start) & (column < start + entries)
        table = jnp.where(hit, 1.0 / 2**level, table)
        start += entries
    return table.astype(jnp.bfloat16)


def split(values):
    high = values.astype(jnp.bfloat16)
    return high, (values - high.astype(jnp.float32)).astype(jnp.bfloat16)


def silu_half(half):
    return half + half * jnp.tanh(half)


def dot(left, right):
    return jnp.dot(left, right, preferred_element_type=jnp.float32)


def encode_block(packed, first, second):
    stacked = jnp.concatenate([packed, packed[:16]], axis=0)
    half = lax.dot_general(stacked, first, (((0,), (0,)), ((), ())), preferred_element_type=jnp.float32)
    return dot(silu_half(half).astype(jnp.bfloat16), second).astype(jnp.bfloat16)


def lookup_plan(view, centre, width_all):
    lane = lax.broadcasted_iota(jnp.int32, (1, 128), 1)
    upper = lane >= 64
    slot = lane & 63
    level = sum((slot >= TAPS * l).astype(jnp.int32) for l in range(1, LEVELS))
    tap = slot - TAPS * level - RADIUS + upper.astype(jnp.int32)

    def by_level(values, dtype):
        out = jnp.full((1, 128), values[0], dtype)
        for l in range(1, LEVELS):
            out = jnp.where(level >= l, jnp.asarray(values[l], dtype), out)
        return out

    factor = by_level([1.0 / 2**l for l in range(LEVELS)], jnp.float32)
    length = by_level([width_all >> l for l in range(LEVELS)], jnp.int32)
    group = by_level([1 << 20, 128, 64, 32], jnp.int32)
    offset = by_level([0, width_all, width_all + 128, width_all + 192], jnp.int32)
    shrink = by_level([0, 0, 64, 96], jnp.int32)
    spot = centre * factor
    floor_value = jnp.floor(spot)
    weight = spot - floor_value
    weight = jnp.where(upper, weight, 1.0 - weight)
    index = floor_value.astype(jnp.int32) + tap
    inside = (index >= 0) & (index < length) & (slot < LEVELS * TAPS)
    weight = jnp.where(inside, weight, 0.0)
    index = jnp.minimum(jnp.maximum(index, 0), length - 1)
    if view:
        index = length - 1 - index
    block = (index >= group).astype(jnp.int32) + (index >= 2 * group).astype(jnp.int32)
    place = offset + index - block * jnp.where(level > 0, group, 0) + 256 * block
    place = place - jnp.where(block == 2, shrink, 0)
    return place, weight


def motion_of(view, query, match, disparity, position, pool, pool_last, weights, scale_bias):
    width_all = match.shape[0]
    scores = lax.dot_general(query, match, (((1,), (1,)), ((), ())), preferred_element_type=jnp.float32)
    rounded = scores.astype(jnp.bfloat16)
    pieces = [scores[:, at : at + 128] for at in range(0, width_all, 128)]
    for at in range(0, width_all - 255, 256):
        pooled = dot(rounded[:, at : at + 256], pool)
        pieces += [pooled[:, :128], pooled[:, 128:]]
    pieces.append(dot(rounded[:, width_all - 128 :], pool_last))
    place, weight = lookup_plan(view, position - disparity, width_all)
    lane = place & 127
    block = place >> 7
    taken = jnp.zeros_like(weight)
    for at, piece in enumerate(pieces):
        values = jnp.take_along_axis(piece, lane, axis=1, mode="promise_in_bounds")
        taken = jnp.where(block == at, values, taken)
    taken = taken * weight
    high = taken.astype(jnp.bfloat16)
    low = (taken - high.astype(jnp.float32)).astype(jnp.bfloat16)
    both = dot(jnp.concatenate([high, low], axis=1), weights)
    half = both[:, :128] + both[:, 128:] + disparity * scale_bias[0:1] + scale_bias[1:2]
    return silu_half(half)


DIRECTIONS = ((-1, 0), (1, 0), (0, -1), (0, 1), (-1, -1), (-1, 1), (1, -1), (1, 1))
EDGE = 16


def sigmoid(values):
    return 0.5 + 0.5 * jnp.tanh(0.5 * values)


def update_kernel(
    voxels_hbm, disparity_hbm, hidden_hbm, context_hbm, first_hbm, bias_hbm, second_hbm, weight_hbm, scale_hbm,
    shift_hbm, gate_hbm, cand_hbm, head_hbm,
    out_hbm, step_hbm,
    voxels_ref, disparity_ref, hidden_ref, context, first_ref, bias_ref, second_ref, weight_ref, scale_ref,
    shift_ref, gate, cand, head_ref,
    packed, arrived, first16, feat, weight64, disp8,
    motion, reset, rows_in, sides_in, wide, blank, out_ref, step_ref,
    local_sem, out_sem, gather_send, gather_recv, halo_send, halo_recv,
):
    views, bins, row_count, cols = voxels_ref.shape
    units = hidden_ref.shape[-1]
    count, bands = lax.axis_size("col"), lax.axis_size("row")
    me, band = lax.axis_index("col"), lax.axis_index("row")

    pairs = {
        "voxels": (voxels_hbm, voxels_ref), "first": (first_hbm, first_ref), "bias": (bias_hbm, bias_ref),
        "second": (second_hbm, second_ref), "weight": (weight_hbm, weight_ref), "scale": (scale_hbm, scale_ref),
        "shift": (shift_hbm, shift_ref), "disparity": (disparity_hbm, disparity_ref),
        "hidden": (hidden_hbm, hidden_ref), "gate": (gate_hbm, gate), "context": (context_hbm, context),
        "cand": (cand_hbm, cand), "head": (head_hbm, head_ref),
    }
    loads = {
        name: pltpu.make_async_copy(source, target, local_sem.at[at])
        for at, (name, (source, target)) in enumerate(pairs.items())
    }
    loads["voxels"].start()

    def inside(dy, dx):
        row, col = band + dy, me + dx
        return (row >= 0) & (row < bands) & (col >= 0) & (col < count)

    barrier = pltpu.get_barrier_semaphore()
    expected = jnp.int32(count - 1)
    for d in range(1, count):
        pl.semaphore_signal(
            barrier, inc=1, device_id={"row": band, "col": lax.rem(me + d, count)}, device_id_type=pl.DeviceIdType.MESH
        )
    for dy, dx in DIRECTIONS:
        if dy:
            there = inside(dy, dx)
            expected = expected + there.astype(jnp.int32)

            @pl.when(there)
            def _(dy=dy, dx=dx):
                pl.semaphore_signal(
                    barrier, inc=1, device_id={"row": band + dy, "col": me + dx}, device_id_type=pl.DeviceIdType.MESH
                )

    for name in list(pairs)[1:]:
        loads[name].start()
    loads["voxels"].wait()

    pieces = [voxels_ref[k // row_count, :, k % row_count, :] for k in range(views * row_count)]
    flat = jnp.concatenate([jnp.concatenate(pieces, axis=1), jnp.ones((16 - bins, 4 * cols), jnp.float32)], axis=0)
    high, low = split(flat)
    packed[...] = jnp.concatenate([high, low], axis=0)

    sources = (hidden_hbm, motion, reset)
    parts = [(0, slice(None))] + [(turn, view) for turn in (1, 2) for view in range(views)]

    def ends(turn, view, q, source):
        dy, dx = DIRECTIONS[q]
        line = 0 if dy < 0 else row_count - 1
        span = pl.ds(0 if dx < 0 else cols - EDGE, EDGE)
        side = 1 if dx < 0 else 0
        if dx == 0:
            return source.at[view, line], rows_in.at[turn, 1 if dy < 0 else 0, view]
        if dy == 0:
            return source.at[view, :, span], sides_in.at[turn, side, view, pl.ds(1, row_count)]
        return source.at[view, line, span], sides_in.at[turn, side, view, row_count + 1 if dy < 0 else 0]

    def place(turn, view):
        return (turn, view) if turn else (0, 0)

    pl.semaphore_wait(barrier, expected)

    gathers = [
        pltpu.make_async_remote_copy(
            src_ref=packed, dst_ref=arrived.at[s - 1], send_sem=gather_send.at[s - 1], recv_sem=gather_recv.at[s - 1],
            device_id={"row": band, "col": lax.rem(me + count - s, count)}, device_id_type=pl.DeviceIdType.MESH,
        )
        for s in range(1, count)
    ]
    for gather in gathers:
        gather.start()

    def halo(turn, view):
        copies = []
        for q, (dy, dx) in enumerate(DIRECTIONS):
            src, dst = ends(turn, view, q, sources[turn])
            copies.append(
                pltpu.make_async_remote_copy(
                    src_ref=src, dst_ref=dst, send_sem=halo_send.at[*place(turn, view), q],
                    recv_sem=halo_recv.at[*place(turn, view), q],
                    device_id={"row": band + dy, "col": me + dx}, device_id_type=pl.DeviceIdType.MESH,
                )
            )
        return copies

    halos = {part: halo(*part) for part in ((turn, 0 if turn == 0 else view) for turn, view in parts) if part[0]}
    halos[0, 0] = halo(0, slice(None))

    def start(part, ways=(-1, 0, 1)):
        for copy, (dy, dx) in zip(halos[part], DIRECTIONS):
            if dy in ways:
                pl.when(inside(dy, dx))(copy.start)

    def arrive(part):
        for copy in halos[part]:
            copy.wait_recv()

    start((0, 0))

    blank[...] = jnp.zeros_like(blank)
    for q, (dy, dx) in enumerate(DIRECTIONS):

        @pl.when(jnp.logical_not(inside(-dy, -dx)))
        def _(q=q):
            for turn, view in parts:
                src, dst = ends(turn, view, q, blank)
                pltpu.make_async_copy(src, dst, halo_recv.at[*place(turn, view), q]).start()

    for name in ("first", "bias", "second", "weight", "scale", "shift", "disparity"):
        loads[name].wait()
    first16[0:bins] = first_ref[...] * 0.5
    first16[bins : bins + 1] = bias_ref[...] * 0.5
    first_high, first_low = split(first16[...])
    first = jnp.concatenate([first_high, first_high, first_low], axis=0)
    weight64[...] = jnp.zeros_like(weight64)
    weight64[0 : LEVELS * TAPS] = weight_ref[...] * 0.5
    high, low = split(weight64[...])
    blank = jnp.zeros_like(low)
    weights = jnp.concatenate(
        [jnp.concatenate([high, low], axis=1)] * 2 + [jnp.concatenate([high, blank], axis=1)] * 2, axis=0
    )
    scale_bias = jnp.concatenate([scale_ref[...] * (0.5 / MAXDISP), shift_ref[...] * 0.5], axis=0)
    disp8[...] = jnp.zeros_like(disp8)
    for k in range(views * row_count):
        disp8[k : k + 1, 0:cols] = disparity_ref[k // row_count, k % row_count : k % row_count + 1, :]
    disparity = disp8[...].T
    pool, pool_last = pooling(256), pooling(128)

    for s in range(count):
        if s:
            gathers[s - 1].wait_recv()
        block = encode_block(arrived[s - 1] if s else packed[...], first, second_ref[...])
        spot = pl.ds(pl.multiple_of(lax.rem(me + s, count) * cols, 32), cols)
        for k in range(views * row_count):
            feat[k, spot, :] = block[k * cols : (k + 1) * cols]

    own = me * cols + lax.broadcasted_iota(jnp.int32, (cols, 1), 0)
    for k in range(views * row_count):
        view, line = k // row_count, k % row_count
        query = feat[k, pl.ds(pl.multiple_of(me * cols, 32), cols), :] * jnp.bfloat16(1.0 / 16)
        position = (count * cols - 1 - own if view else own).astype(jnp.float32)
        other = (views - 1 - view) * row_count + line
        motion[view, line] = motion_of(
            view, query, feat[other], disparity[:cols, k : k + 1], position, pool, pool_last, weights, scale_bias
        ).astype(jnp.bfloat16)
        if line == 0:
            start((1, view), (-1,))
        if line == row_count - 1:
            start((1, view), (0, 1))

    slot = lax.broadcasted_iota(jnp.int32, (EDGE, units), 0)

    def widen(turn, view, source):
        for line in range(row_count + 2):
            if line == 0:
                centre = rows_in[turn, 0, view]
            elif line == row_count + 1:
                centre = rows_in[turn, 1, view]
            else:
                centre = source[view, line - 1]
            left = sides_in[turn, 0, view, line].astype(jnp.float32)
            right = sides_in[turn, 1, view, line].astype(jnp.float32)
            edge = jnp.where(slot == EDGE - 1, left, right)
            ring = jnp.concatenate([centre.astype(jnp.float32), edge], axis=0)
            before = pltpu.roll(ring, 1, axis=0)[:cols]
            after = pltpu.roll(ring, cols + EDGE - 1, axis=0)[:cols]
            if view:
                before, after = after, before
            wide[turn, view, line, :, 0:units] = before.astype(jnp.bfloat16)
            wide[turn, view, line, :, units : 2 * units] = centre
            wide[turn, view, line, :, 2 * units :] = after.astype(jnp.bfloat16)

    def convolve(turn, first_view, kernel, part, channels, many=1):
        window = jnp.concatenate(
            [
                wide[turn, first_view : first_view + many, a : a + row_count].reshape(-1, 3 * units)
                for a in range(3)
            ],
            axis=1,
        )
        taps = jnp.concatenate(
            [kernel[a, b, part * units : (part + 1) * units, channels] for a in range(3) for b in range(3)], axis=0
        )
        return dot(window, taps)

    def flat_rows(values):
        return values.reshape(row_count * cols, values.shape[-1]).astype(jnp.float32)

    loads["hidden"].wait()
    loads["gate"].wait()
    arrive((0, 0))
    for view in range(views):
        widen(0, view, hidden_ref)
    early, late = slice(units, 2 * units), slice(0, units)
    reset_terms = convolve(0, 0, gate, 0, early, views).reshape(views, row_count * cols, units)
    loads["context"].wait()
    for view in range(views):
        arrive((1, view))
        widen(1, view, motion)
        terms = reset_terms[view] + convolve(1, view, gate, 1, early)
        kept = sigmoid(terms + flat_rows(context[view, :, :, early])) * flat_rows(hidden_ref[view])
        reset[view] = kept.astype(jnp.bfloat16).reshape(row_count, cols, units)
        start((2, view))
    loads["cand"].wait()
    loads["head"].wait()
    open_terms = convolve(0, 0, gate, 0, late, views) + convolve(1, 0, gate, 1, late, views)
    opened = sigmoid(open_terms.reshape(views, row_count * cols, units) + context[:, :, :, late].reshape(
        views, row_count * cols, units).astype(jnp.float32))
    cand_terms = convolve(1, 0, cand, 1, late, views).reshape(views, row_count * cols, units)
    exits = [pltpu.make_async_copy(out_ref.at[view], out_hbm.at[view], out_sem.at[view]) for view in range(views)]
    exits.append(pltpu.make_async_copy(step_ref, step_hbm, out_sem.at[views]))
    for view in range(views):
        arrive((2, view))
        widen(2, view, reset)
        terms = cand_terms[view] + convolve(2, view, cand, 0, late)
        candidate = jnp.tanh(terms + flat_rows(context[view, :, :, 2 * units :]))
        state = flat_rows(hidden_ref[view])
        updated = ((1.0 - opened[view]) * state + opened[view] * candidate).astype(jnp.bfloat16)
        out_ref[view] = updated.reshape(row_count, cols, units)
        for line in range(row_count):
            step_ref[view, line : line + 1, :] = lax.dot_general(
                head_ref[...], updated[line * cols : (line + 1) * cols], (((1,), (1,)), ((), ())),
                preferred_element_type=jnp.float32,
            )
        exits[view].start()
    exits[views].start()
    for gather in gathers:
        gather.wait_send()
    for q, (dy, dx) in enumerate(DIRECTIONS):

        @pl.when(inside(dy, dx))
        def _(q=q):
            for copies in halos.values():
                copies[q].wait_send()

    for leave in exits:
        leave.wait()


def hand_out(state_in, step_in, state_out, step_out, state, step, sem):
    views = state.shape[0]
    arrivals = [pltpu.make_async_copy(state_in.at[view], state.at[view], sem.at[0, view]) for view in range(views)]
    exits = [pltpu.make_async_copy(state.at[view], state_out.at[view], sem.at[1, view]) for view in range(views)]
    arrivals.append(pltpu.make_async_copy(step_in, step, sem.at[0, views]))
    exits.append(pltpu.make_async_copy(step, step_out, sem.at[1, views]))
    for copy in arrivals:
        copy.start()
    for arrival, leave in zip(arrivals, exits):
        arrival.wait()
        leave.start()
    for leave in exits:
        leave.wait()


def local(
    voxels, disparity, hidden, context, embed_first, embed_bias, embed_second, motion_weight, motion_scale,
    motion_bias, gate_kernel, candidate_kernel, head_weight,
):
    views, bins, row_count, cols = voxels.shape
    units = hidden.shape[-1]
    channels = embed_second.shape[0]
    count = lax.axis_size("col")
    pixels = views * row_count * cols
    hbm = pl.BlockSpec(memory_space=pltpu.HBM)
    operands = (
        voxels, disparity, hidden, context, embed_first, embed_bias[None], embed_second, motion_weight,
        motion_scale[None], motion_bias[None], gate_kernel, candidate_kernel, head_weight[None],
    )
    shapes = (
        jax.ShapeDtypeStruct(hidden.shape, jnp.bfloat16),
        jax.ShapeDtypeStruct(disparity.shape, jnp.float32),
    )
    results = pl.pallas_call(
        update_kernel,
        out_shape=shapes,
        in_specs=[hbm] * len(operands),
        out_specs=(hbm, hbm),
        scratch_shapes=[pltpu.VMEM(operand.shape, operand.dtype) for operand in operands]
        + [
            pltpu.VMEM((32, pixels), jnp.bfloat16),
            pltpu.VMEM((count - 1, 32, pixels), jnp.bfloat16),
            pltpu.VMEM((16, channels), jnp.float32),
            pltpu.VMEM((views * row_count, count * cols, channels), jnp.bfloat16),
            pltpu.VMEM((64, units), jnp.float32),
            pltpu.VMEM((8, 256), jnp.float32),
            pltpu.VMEM(hidden.shape, jnp.bfloat16),
            pltpu.VMEM(hidden.shape, jnp.bfloat16),
            pltpu.VMEM((3, 2, views, cols, units), jnp.bfloat16),
            pltpu.VMEM((3, 2, views, row_count + 2, EDGE, units), jnp.bfloat16),
            pltpu.VMEM((3, views, row_count + 2, cols, 3 * units), jnp.bfloat16),
            pltpu.VMEM(hidden.shape, jnp.bfloat16),
            pltpu.VMEM(hidden.shape, jnp.bfloat16),
            pltpu.VMEM(disparity.shape, jnp.float32),
            pltpu.SemaphoreType.DMA((len(operands),)),
            pltpu.SemaphoreType.DMA((views + 1,)),
            pltpu.SemaphoreType.DMA((count - 1,)),
            pltpu.SemaphoreType.DMA((count - 1,)),
            pltpu.SemaphoreType.DMA((3, views, 8)),
            pltpu.SemaphoreType.DMA((3, views, 8)),
        ],
        compiler_params=pltpu.CompilerParams(
            collective_id=0, has_side_effects=True, vmem_limit_bytes=64 * 2**20
        ),
    )(*operands)
    return pl.pallas_call(
        hand_out,
        out_shape=shapes,
        in_specs=[hbm] * 2,
        out_specs=(hbm, hbm),
        scratch_shapes=[
            pltpu.VMEM(hidden.shape, jnp.bfloat16),
            pltpu.VMEM(disparity.shape, jnp.float32),
            pltpu.SemaphoreType.DMA((2, views + 1)),
        ],
        compiler_params=pltpu.CompilerParams(vmem_limit_bytes=64 * 2**20),
    )(*results)


def solution(mesh):
    tile = P(None, ("pair", "row"), "col")
    in_specs = (P(None, None, ("pair", "row"), "col"),) + (tile,) * 3 + (P(),) * 9
    return jax.shard_map(local, mesh=mesh, in_specs=in_specs, out_specs=(tile, tile), check_vma=False)
```
